128 devices in a mesh: lat: 4 (over x), lon: 32 (over y, z, core).
Axes of the slice: x: 4, y: 4, z: 4, core: 2. Of those that a mesh axis runs over, the one named last changes fastest.
Arguments:
- velocity_old: float32 [2, 1024, 8192], P(None, 'lat', 'lon'), may hold values from -3 to 3
- wind_stress: float32 [2, 1024, 8192], P(None, 'lat', 'lon'), may hold values from -3 to 3
- strength: float32 [1024, 8192], P('lat', 'lon'), may hold values from 0.3 to 3
- ice_mass: float32 [1024, 8192], P('lat', 'lon'), may hold values from 0.5 to 2
- ice_mask: int32 [8, 64], P('lat', 'lon'), may hold values from 0 to 1, as said below
- block_owner: int32 [8, 64], P('lat', 'lon'), may hold values from 0 to 3, as said below
- block_slot: int32 [8, 64], P('lat', 'lon'), may hold values from 0 to 1
Outputs:
- velocity: float32 [2, 1024, 8192], P(None, 'lat', 'lon')
- held_velocity: float32 [8, 32, 2, 128, 128], P('lat', 'lon')
The draws below stay inside these ranges and needn't reach their ends.
Inputs may be any that keep to these rules, and one draw needn't show every extreme that they name: `ice_mask`: in every group of 2 block columns of one longitude tile, exactly 8 blocks are ice, among them all blocks of the first 2 block rows. Over the ice blocks of one such group, block_owner * 2 + block_slot takes each value 0 to 7 exactly once; on open-water blocks both are arbitrary within their ranges.
All inputs are finite; a program needn't handle non-finite values.
Results may differ from the reference program's by a relative error of at most 0.0008.
Values sent between devices are 32-bit elements; how exact they have to be, the bound alone decides.
A program may use at most 128 MiB of HBM per device.

```python
import math
import jax
import jax.numpy as jnp

BS = 128
BR = 2
BC = 2
KRYLOV = 5
NEWTON = 2
CAP = 2
HELD = 8
NBR = 8
NBC = 64
NY = 1024
NX = 8192
N_LON = 32


def deal_ranks(key):
    lat_tiles = NBR // BR
    lon_tiles = NBC // BC
    tile_size = BR * BC
    group_size = lat_tiles * tile_size
    chosen = lat_tiles * CAP
    score_key, order_key = jax.random.split(key)
    tile_index = jnp.arange(group_size) // tile_size
    noise_draw = jax.random.randint(score_key, (lon_tiles, group_size), 0, 1024)
    priority = noise_draw - 256 * tile_index[None, :] + jnp.where(tile_index == 0, 65536, 0)[None, :]
    distinct = priority * group_size + jnp.arange(group_size)[None, :]
    ordering = jnp.argsort(-distinct, axis=1)
    position = jnp.argsort(ordering, axis=1)
    ice_flag = (position < chosen).astype(jnp.int32)
    shuffle = jax.random.randint(order_key, (lon_tiles, group_size), 0, 65536)
    deal_score = (1 - ice_flag) * (1 << 28) + shuffle * group_size + jnp.arange(group_size)[None, :]
    deal_rank = jnp.argsort(jnp.argsort(deal_score, axis=1), axis=1).astype(jnp.int32)
    return (ice_flag, deal_rank)


def to_grid(values):
    lat_tiles = NBR // BR
    lon_tiles = NBC // BC
    shaped = values.reshape(lon_tiles, lat_tiles, BR, BC)
    return shaped.transpose(1, 2, 0, 3).reshape(NBR, NBC).astype(jnp.int32)


def draw_ice_mask(key, part):
    ice_flag, deal_rank = deal_ranks(key)
    return to_grid(ice_flag)


def draw_block_owner(key, part):
    ice_flag, deal_rank = deal_ranks(key)
    key = jax.random.fold_in(key, 11)
    spare = jax.random.randint(key, ice_flag.shape, 0, NBR // BR)
    return to_grid(jnp.where(ice_flag == 1, deal_rank // CAP, spare))


def draw_block_slot(key, part):
    ice_flag, deal_rank = deal_ranks(key)
    key = jax.random.fold_in(key, 12)
    spare = jax.random.randint(key, ice_flag.shape, 0, CAP)
    return to_grid(jnp.where(ice_flag == 1, deal_rank % CAP, spare))


def draw_wind_stress(key, part):
    key = jax.random.fold_in(key, 7)
    shape = (2, NY, NX)
    values = jnp.clip(jax.random.normal(key, shape, jnp.float32), -3.0, 3.0)
    return values


def level_of(rng, dims, shards, low, high):
    level, own = 1.0, jax.random.fold_in(rng, 6)
    for axis_at, parts in shards:
        steps = jnp.exp(jax.random.uniform(jax.random.fold_in(own, axis_at), (parts,), jnp.float32, low / len(shards), high / len(shards)))
        level = level * jnp.repeat(steps, dims[axis_at] // parts).reshape([-1 if axis == axis_at else 1 for axis in range(len(dims))])
    return level


def bell_draw(own_key, extent, width, reach, shards=(), dtype=jnp.bfloat16):
    gain = level_of(own_key, extent, shards, -0.22, 0.18) if shards else 1.0
    drawn = jax.random.normal(own_key, extent, jnp.float32) * width * gain
    return jnp.minimum(jnp.maximum(drawn, -reach), reach).astype(dtype)


def setup_inputs(seed: int = 0) -> dict:
    keys = jax.random.split(jax.random.key(seed), 8)
    return {
        "velocity_old": bell_draw(keys[0], (2, NY, NX), 0.5, 3.0, ((1, 4), (2, 32)), jnp.float32),
        "wind_stress": draw_wind_stress(jax.random.fold_in(keys[7], 71), 0),
        "strength": jnp.clip(jnp.exp(math.log(3.0) - 2.3025851 * jax.random.uniform(keys[2], (NY, NX), jnp.float32) ** level_of(keys[2], (NY, NX), ((0, 4), (1, 32)), -0.2, 0.2)), 0.3, 3.0),
        "ice_mass": jnp.clip(jnp.exp(math.log(2.0) - 1.3862944 * jax.random.uniform(keys[3], (NY, NX), jnp.float32) ** level_of(keys[3], (NY, NX), ((0, 4), (1, 32)), -0.2, 0.2)), 0.5, 2.0),
        "ice_mask": draw_ice_mask(jax.random.fold_in(keys[7], 71), 0),
        "block_owner": draw_block_owner(jax.random.fold_in(keys[7], 71), 0),
        "block_slot": draw_block_slot(jax.random.fold_in(keys[7], 71), 0),
    }


dmin_sq = 0.04
ellipse_sq = 4.0
drag_coef = 0.5
coriolis = 0.3
tiny_sq = 1e-06

def slope_x(field):
    return (field[..., 1:-1, 2:] - field[..., 1:-1, :-2]) * 0.5

def slope_y(field):
    return (field[..., 2:, 1:-1] - field[..., :-2, 1:-1]) * 0.5

def strain_rates(flow_wide):
    flow_east = flow_wide[..., 0, :, :]
    flow_north = flow_wide[..., 1, :, :]
    return (slope_x(flow_east), slope_y(flow_north), 0.5 * (slope_y(flow_east) + slope_x(flow_north)))

def viscosities(widened):
    normal_xx, normal_yy, shear_rate = strain_rates(widened[..., 0:2, :, :])
    pressure_mid = widened[..., 2, 1:-1, 1:-1]
    strain_sum = normal_xx + normal_yy
    differ = normal_xx - normal_yy
    squared = strain_sum * strain_sum + (differ * differ + 4.0 * shear_rate * shear_rate) / ellipse_sq
    delta_rate = jnp.sqrt(squared + dmin_sq)
    bulk_visc = pressure_mid / (2.0 * delta_rate)
    visc_slope = bulk_visc / (2.0 * delta_rate * delta_rate)
    return (bulk_visc, visc_slope, strain_sum, differ, shear_rate, pressure_mid)

def divergence(stress_xx, stress_yy, stress_xy):
    return (slope_x(stress_xx) + slope_y(stress_xy), slope_x(stress_xy) + slope_y(stress_yy))

def stress_force(bulk_visc, strain_sum, differ, shear_rate, pressure_mid):
    shear_visc = bulk_visc / ellipse_sq
    return divergence(bulk_visc * strain_sum + shear_visc * differ - 0.5 * pressure_mid, bulk_visc * strain_sum - shear_visc * differ - 0.5 * pressure_mid, 2.0 * shear_visc * shear_rate)

def tangent_force(wide_dir, bulk_visc, visc_slope, strain_sum, differ, shear_rate):
    change_xx, change_yy, change_shear = strain_rates(wide_dir)
    change_total = change_xx + change_yy
    change_differ = change_xx - change_yy
    change_squared = 2.0 * strain_sum * change_total + (2.0 * differ * change_differ + 8.0 * shear_rate * change_shear) / ellipse_sq
    change_bulk = -visc_slope * change_squared
    return divergence(change_bulk * (strain_sum + differ / ellipse_sq) + bulk_visc * (change_total + change_differ / ellipse_sq), change_bulk * (strain_sum - differ / ellipse_sq) + bulk_visc * (change_total - change_differ / ellipse_sq), 2.0 * (change_bulk * shear_rate + bulk_visc * change_shear) / ellipse_sq)

def inertia(flow_now, ice_mass, force_east, force_north):
    flow_east = flow_now[..., 0, :, :]
    flow_north = flow_now[..., 1, :, :]
    along_first = ice_mass * flow_east - coriolis * ice_mass * flow_north + drag_coef * flow_east - force_east
    along_second = ice_mass * flow_north + coriolis * ice_mass * flow_east + drag_coef * flow_north - force_north
    return jnp.stack([along_first, along_second], axis=-3)

def least_squares(hessen, initial_norm):
    upper = hessen
    target_vec = jnp.zeros((KRYLOV + 1,), jnp.float32).at[0].set(initial_norm)
    for column in range(KRYLOV):
        top_entry = upper[column, column]
        below_entry = upper[column + 1, column]
        radius = jnp.sqrt(top_entry * top_entry + below_entry * below_entry)
        cosine = top_entry / radius
        sine_part = below_entry / radius
        first_row = upper[column]
        second_row = upper[column + 1]
        upper = upper.at[column].set(cosine * first_row + sine_part * second_row)
        upper = upper.at[column + 1].set(cosine * second_row - sine_part * first_row)
        first_entry = target_vec[column]
        second_entry = target_vec[column + 1]
        target_vec = target_vec.at[column].set(cosine * first_entry + sine_part * second_entry)
        target_vec = target_vec.at[column + 1].set(cosine * second_entry - sine_part * first_entry)
    weights = jnp.zeros((KRYLOV,), jnp.float32)
    for column in reversed(range(KRYLOV)):
        known = jnp.sum(upper[column, column + 1:] * weights[column + 1:])
        weights = weights.at[column].set((target_vec[column] - known) / upper[column, column])
    return weights

def inner_product(first_vec, second_vec):
    return jnp.sum(first_vec * second_vec)

def krylov_solve(linear_map, target_vec):
    initial_norm = jnp.sqrt(inner_product(target_vec, target_vec) + tiny_sq)
    krylov_basis = [target_vec / initial_norm]
    hessen = jnp.zeros((KRYLOV + 1, KRYLOV), jnp.float32)
    for column in range(KRYLOV):
        mapped = linear_map(krylov_basis[column])
        coeffs = jnp.stack([inner_product(vector, mapped) for vector in krylov_basis])
        for previous in range(column + 1):
            mapped = mapped - coeffs[previous] * krylov_basis[previous]
        length = jnp.sqrt(inner_product(mapped, mapped) + tiny_sq)
        hessen = hessen.at[:column + 1, column].set(coeffs).at[column + 1, column].set(length)
        krylov_basis.append(mapped / length)
    weights = least_squares(hessen, initial_norm)
    update = weights[0] * krylov_basis[0]
    for column in range(1, KRYLOV):
        update = update + weights[column] * krylov_basis[column]
    return update

def solve_newton(flow_now, flow_old, wind_stress, pressure, ice_mass, ice_weight, widen):
    for newton_step in range(NEWTON):
        widened = widen(jnp.concatenate([flow_now, pressure[..., None, :, :]], axis=-3))
        bulk_visc, visc_slope, strain_sum, differ, shear_rate, pressure_mid = viscosities(widened)
        force_east, force_north = stress_force(bulk_visc, strain_sum, differ, shear_rate, pressure_mid)
        residual = ice_weight * (inertia(flow_now, ice_mass, force_east, force_north) - ice_mass[..., None, :, :] * flow_old - wind_stress)

        def linear_map(direction):
            change_east, change_north = tangent_force(widen(direction), bulk_visc, visc_slope, strain_sum, differ, shear_rate)
            return ice_weight * inertia(direction, ice_mass, change_east, change_north)
        flow_now = flow_now + krylov_solve(linear_map, -residual)
    return flow_now

def widen_grid(field):
    wrapped = jnp.pad(field, ((0, 0), (0, 0), (2, 2)), mode='wrap')
    return jnp.pad(wrapped, ((0, 0), (2, 2), (0, 0)))

def reference(velocity_old, wind_stress, strength, ice_mass, ice_mask, block_owner, block_slot):
    ice_float = ice_mask.astype(jnp.float32)
    ice_weight = jnp.repeat(jnp.repeat(ice_float, BS, axis=0), BS, axis=1)
    flow_now = solve_newton(velocity_old * ice_weight, velocity_old, wind_stress, strength * ice_weight, ice_mass, ice_weight, widen_grid)
    blocks = flow_now.reshape(2, NBR, BS, NBC, BS).transpose(1, 3, 0, 2, 4)
    column_group = (jnp.arange(NBC) // BC).astype(jnp.int32)
    target_row = ((block_owner * CAP + block_slot) * N_LON + column_group[None, :]).astype(jnp.int32)
    weighted = blocks * ice_float[:, :, None, None, None]
    held = jnp.zeros((HELD * N_LON, 2, BS, BS), jnp.float32).at[target_row.reshape(-1)].add(weighted.reshape(NBR * NBC, 2, BS, BS))
    return (flow_now, held.reshape(HELD, N_LON, 2, BS, BS))
```

```python
import functools

import jax
import jax.numpy as jnp
from jax import lax
from jax.experimental import pallas as pl
from jax.experimental.pallas import tpu as pltpu
from jax.sharding import PartitionSpec as P

MESH = pl.DeviceIdType.MESH
F32 = jnp.float32

KRYLOV = 5
TINY_SQ = 1e-6
LAT = 4
LON = 32

ROWS = 320
TOP = 32
BOT = 288
HALO = 24
OWN_STRIPS = 32

WIDTHS = (22, 22, 22, 20, 20, 20)
OFFSETS = (0, 22, 44, 66, 86, 106)

N_DOTS = 21
N_SUMS = 24


def lanes(shape):
    return lax.broadcasted_iota(jnp.int32, shape, len(shape) - 1)


def rows8(start):
    return pl.ds(start, 8)


def diff_x(f):
    lane = lanes((1, 8, 128))
    right = pltpu.roll(f, 127, 2)
    left = pltpu.roll(f, 1, 2)
    right_next = jnp.concatenate([right[1:], right[:1]], axis=0)
    left_next = jnp.concatenate([left[2:], left[:2]], axis=0)
    return jnp.where(lane == 127, right_next, right) - jnp.where(lane == 0, left_next, left)


def diff_x_rough(f):
    return pltpu.roll(f, 127, 2) - pltpu.roll(f, 1, 2)


def coefficients(sum_rate, differ, shear, pressure):
    q = 0.25 * (sum_rate * sum_rate) + 0.0625 * (differ * differ + shear * shear)
    inv = lax.rsqrt(q + 0.04)
    bulk = 0.5 * pressure * inv
    weight = inv * jnp.sqrt(0.5 * bulk)
    eighth = 0.125 * weight
    return 0.5 * bulk, 0.125 * bulk, (0.5 * weight) * sum_rate, eighth * differ, eighth * shear


def spectrum_sums(m2, gs, gf, ge, mass, turn):
    diag = mass + 1.5 * m2 - (gs * gs + gf * gf + ge * ge)
    c11 = 2.5 * m2 - 2.0 * (gs + gf) * (gs + gf)
    c22 = 2.5 * m2 - 2.0 * (gs - gf) * (gs - gf)
    c33 = 2.0 * m2 - 8.0 * ge * ge
    spread = diag * diag + turn * turn + 0.0625 * (c11 * c11 + c22 * c22) + 0.03125 * (c33 * c33)
    return diag, spread


def splat(row, index):
    return jnp.broadcast_to(row[:, index : index + 1], (1, 128))


def wide(row):
    return jnp.broadcast_to(row, (8, 128))


def small_solve(gram, mid, rho):
    def dot(u, gv):
        total = None
        for x, y in zip(u, gv):
            if x is not None:
                total = x * y if total is None else total + x * y
        return total

    def times_gram(u, count):
        return [dot(u, [gram[i][j] for j in range(6)]) for i in range(count)]

    def apply(c):
        out = [None] * 6
        for k, x in enumerate(c):
            if x is None:
                continue
            if k < 5:
                terms = [(k + 1, x), (k, mid * x)]
                if k > 0:
                    terms.append((k - 1, rho[k] * x))
                for at, term in terms:
                    out[at] = term if out[at] is None else out[at] + term
        return out

    beta = jnp.sqrt(gram[0][0] + TINY_SQ)
    basis = [[1.0 / beta] + [None] * 5]
    upper = []
    cosines, sines = [], []
    target = [beta]
    for j in range(KRYLOV):
        u = apply(basis[j])
        gu = times_gram(u, j + 2)
        coeffs = [dot(basis[i][: j + 2], gu) for i in range(j + 1)]
        for i in range(j + 1):
            u = [
                x if y is None else x - coeffs[i] * y
                for x, y in zip(u, basis[i])
            ]
        gu = times_gram(u, j + 2)
        square = jnp.maximum(dot(u[: j + 2], gu), 0.0)
        length = jnp.sqrt(square + TINY_SQ)
        inv_length = 1.0 / length
        basis.append([None if x is None else x * inv_length for x in u])
        column = coeffs + [length]
        for i in range(j):
            a, b = column[i], column[i + 1]
            column[i] = cosines[i] * a + sines[i] * b
            column[i + 1] = cosines[i] * b - sines[i] * a
        a, b = column[j], column[j + 1]
        inv_radius = 1.0 / jnp.sqrt(a * a + b * b)
        cosine, sine = a * inv_radius, b * inv_radius
        cosines.append(cosine)
        sines.append(sine)
        column[j] = cosine * a + sine * b
        upper.append(column[: j + 1])
        target.append(-sine * target[j])
        target[j] = cosine * target[j]
    weights = [None] * KRYLOV
    for j in reversed(range(KRYLOV)):
        known = target[j]
        for k in range(j + 1, KRYLOV):
            known = known - upper[k][j] * weights[k]
        weights[j] = known / upper[j][j]
    out = []
    for k in range(KRYLOV):
        total = None
        for j in range(k, KRYLOV):
            term = weights[j] * basis[j][k]
            total = term if total is None else total + term
        out.append(total)
    return out


def kernel(
    ice_ref, owner_ref, slot_ref, vel_ref, wind_ref, strength_ref, mass_ref,
    out_ref, held_ref,
    st_vel, st_wind, st_strength, st_mass,
    fields, local, coef, stress, krylov,
    pack_e, pack_w, got_l, got_r, sums,
    buf_a, buf_b, send_blocks, recv_blocks, held_buf,
    in_sem, halo_send, halo_recv, ar_send, ar_recv, held_send, held_recv, out_sem,
):
    lat, lon = lax.axis_index("lat"), lax.axis_index("lon")
    north, south = lax.rem(lat + LAT - 1, LAT), lax.rem(lat + 1, LAT)
    east, west = lax.rem(lon + 1, LON), lax.rem(lon + LON - 1, LON)
    core = lax.rem(lon, 2)
    chip = lon // 2
    rank_a = lat * 2 + core
    rank_b = chip

    peers_a = []
    for i in (4, 5, 2, 3, 6, 7, 1):
        other = lax.rem(rank_a + i, 8)
        peers_a.append((other // 2, chip * 2 + lax.rem(other, 2)))
    peers_b = []
    for i in (10, 9, 11, 6, 8, 2, 14, 7, 5, 13, 1, 3, 15, 4, 12):
        peers_b.append((lat, lax.rem(rank_b + i, 16) * 2 + core))
    halo_peers = [(lat, east), (lat, west), (north, east), (north, west), (south, east), (south, west)]

    barrier = pltpu.get_barrier_semaphore()
    greeted = peers_b + peers_a + halo_peers
    for peer in greeted:
        pl.semaphore_signal(barrier, inc=1, device_id=peer, device_id_type=MESH)

    loads = []
    for t in range(2):
        cols = pl.ds(128 * t, 128)
        loads.append(pltpu.make_async_copy(vel_ref.at[:, :, cols], st_vel.at[:, t], in_sem.at[t]))
        loads.append(pltpu.make_async_copy(wind_ref.at[:, :, cols], st_wind.at[:, t], in_sem.at[2 + t]))
        loads.append(pltpu.make_async_copy(strength_ref.at[:, cols], st_strength.at[t], in_sem.at[4 + t]))
        loads.append(pltpu.make_async_copy(mass_ref.at[:, cols], st_mass.at[t], in_sem.at[6 + t]))
    for copy in loads:
        copy.start()
    for copy in loads:
        copy.wait()

    lane8 = lanes((8, 128))
    ice = [[ice_ref[i, j].astype(F32) for j in range(2)] for i in range(2)]
    for half in range(2):

        def prepare(s, carry, half=half):
            src = pl.multiple_of(8 * s, 8)
            dst = pl.multiple_of(TOP + 8 * s, 8)
            for t in range(2):
                w = ice[half][t]
                mass = st_mass[t, rows8(src), :] * w
                v_e = st_vel[0, t, rows8(src), :]
                v_n = st_vel[1, t, rows8(src), :]
                values = (
                    v_e * w,
                    v_n * w,
                    st_strength[t, rows8(src), :] * w,
                    mass,
                    mass * v_e + w * st_wind[0, t, rows8(src), :],
                    mass * v_n + w * st_wind[1, t, rows8(src), :],
                )
                for f in range(6):
                    fields[f, t, rows8(dst), :] = values[f]
                local[0, t, rows8(dst), :] = mass + 0.5 * w
                local[1, t, rows8(dst), :] = 0.3 * mass
                local[2, t, rows8(dst), :] = jnp.zeros((8, 128), F32) + 0.5 * w
                packed = None
                for f in range(6):
                    turn = (OFFSETS[f] if t == 0 else OFFSETS[f] + WIDTHS[f]) % 128
                    rolled = values[f] if turn == 0 else pltpu.roll(values[f], turn, 1)
                    packed = rolled if f == 0 else jnp.where(lane8 >= OFFSETS[f], rolled, packed)
                (pack_w if t == 0 else pack_e)[rows8(src), :] = packed
            return carry

        lax.fori_loop(16 * half, 16 * half + 16, prepare, 0)

    pl.semaphore_wait(barrier, len(greeted))

    own_top, own_bot = pl.ds(TOP, HALO), pl.ds(BOT - HALO, HALO)
    halo_top, halo_bot = pl.ds(TOP - HALO, HALO), pl.ds(BOT, HALO)
    own_rows = pl.ds(TOP, 256)
    src_top, src_bot = pl.ds(0, HALO), pl.ds(256 - HALO, HALO)
    plan = [
        (fields.at[:, pl.ds(0, 2), own_top, :], fields.at[:, pl.ds(0, 2), halo_bot, :], (north, lon)),
        (fields.at[:, pl.ds(0, 2), own_bot, :], fields.at[:, pl.ds(0, 2), halo_top, :], (south, lon)),
        (pack_e.at[src_top, :], got_l.at[halo_bot, :], (north, east)),
        (pack_w.at[src_top, :], got_r.at[halo_bot, :], (north, west)),
        (pack_e.at[src_bot, :], got_l.at[halo_top, :], (south, east)),
        (pack_w.at[src_bot, :], got_r.at[halo_top, :], (south, west)),
        (pack_e, got_l.at[own_rows, :], (lat, east)),
        (pack_w, got_r.at[own_rows, :], (lat, west)),
    ]
    halo_copies = []
    for i, (src, dst, peer) in enumerate(plan):
        copy = pltpu.make_async_remote_copy(
            src_ref=src, dst_ref=dst, send_sem=halo_send.at[i], recv_sem=halo_recv.at[i],
            device_id=peer, device_id_type=MESH,
        )
        copy.start()
        halo_copies.append(copy)

    def reduce_a_start(inst, row):
        buf_a[inst, rank_a] = row
        for peer in peers_a:
            pltpu.make_async_remote_copy(
                src_ref=buf_a.at[inst, rank_a], dst_ref=buf_a.at[inst, rank_a],
                send_sem=ar_send.at[inst, 0], recv_sem=ar_recv.at[inst, 0],
                device_id=peer, device_id_type=MESH,
            ).start()

    def reduce_b_start(inst):
        waited = buf_a.at[inst, pl.ds(0, 7)]
        pltpu.make_async_copy(waited, waited, ar_recv.at[inst, 0]).wait()
        row = buf_a[inst, 0]
        for i in range(1, 8):
            row = row + buf_a[inst, i]
        buf_b[inst, rank_b] = row
        for peer in peers_b:
            pltpu.make_async_remote_copy(
                src_ref=buf_b.at[inst, rank_b], dst_ref=buf_b.at[inst, rank_b],
                send_sem=ar_send.at[inst, 1], recv_sem=ar_recv.at[inst, 1],
                device_id=peer, device_id_type=MESH,
            ).start()

    def reduce_end(inst):
        waited = buf_b.at[inst, pl.ds(0, 15)]
        pltpu.make_async_copy(waited, waited, ar_recv.at[inst, 1]).wait()
        parts = [buf_b[inst, i] for i in range(16)]
        while len(parts) > 1:
            parts = [x + y for x, y in zip(parts[::2], parts[1::2])]
        return parts[0]

    def put_sum(index, acc):
        sums[index : index + 1, :] = jnp.sum(acc, axis=0, keepdims=True)

    def packed_sums(count):
        m = sums[0:count, :]
        total = jnp.sum(m, axis=1, keepdims=True)
        sub = lax.broadcasted_iota(jnp.int32, (count, 128), 0)
        spread = jnp.where(lanes((count, 128)) == sub, total, 0.0)
        return jnp.sum(spread, axis=0, keepdims=True)

    def estimate_pass(alpha):
        both = pl.ds(0, 2)

        def at(c, r):
            flow = fields[c, both, rows8(r), :]
            return flow if alpha is None else flow + alpha * krylov[0, c, both, rows8(r), :]

        def body(i, carry):
            diag_acc, spread_acc, ice_acc = carry
            r = pl.multiple_of(TOP + 8 + 16 * i, 8)
            x_e, x_n = diff_x_rough(at(0, r)), diff_x_rough(at(1, r))
            y_e, y_n = at(0, r + 1) - at(0, r - 1), at(1, r + 1) - at(1, r - 1)
            m2, _, gs, gf, ge = coefficients(x_e + y_n, x_e - y_n, y_e + x_n, fields[2, both, rows8(r), :])
            diag, spread = spectrum_sums(
                m2, gs, gf, ge, local[0, both, rows8(r), :], local[1, both, rows8(r), :]
            )
            weight = local[2, both, rows8(r), :]
            return (
                diag_acc + (diag[0] + diag[1]),
                spread_acc + (spread[0] + spread[1]),
                ice_acc + 2.0 * (weight[0] + weight[1]),
            )

        zero = jnp.zeros((8, 128), F32)
        return lax.fori_loop(0, 15, body, (zero, zero, zero))

    def basis_of(row, at):
        diag, spread, count = splat(row, at), splat(row, at + 1), splat(row, at + 2)
        inv = 1.0 / jnp.maximum(count, 1.0)
        mid = diag * inv
        return mid, jnp.maximum(spread * inv - mid * mid, 0.01)

    for i, acc in enumerate(estimate_pass(None)):
        put_sum(i, acc)
    reduce_a_start(0, packed_sums(8))

    for copy in halo_copies:
        copy.wait_recv()

    keep_top = jnp.where(lat == 0, 0.0, 1.0).astype(F32)
    keep_bot = jnp.where(lat == LAT - 1, 0.0, 1.0).astype(F32)

    def put_local(t, r, mass):
        w = jnp.where(mass > 0.0, 1.0, 0.0)
        local[0, t, rows8(r), :] = mass + 0.5 * w
        local[1, t, rows8(r), :] = 0.3 * mass
        local[2, t, rows8(r), :] = 0.5 * w

    def unpack(lo, hi, keep):
        def body(s, carry):
            r = pl.multiple_of(8 + 8 * s, 8)
            left, right = got_l[rows8(r), :], got_r[rows8(r), :]
            for f in range(6):
                turn_l = (128 - OFFSETS[f] - WIDTHS[f]) % 128
                turn_r = (128 - OFFSETS[f]) % 128
                from_l = left if turn_l == 0 else pltpu.roll(left, turn_l, 1)
                from_r = right if turn_r == 0 else pltpu.roll(right, turn_r, 1)
                merged = jnp.where(lane8 < 64, from_r, from_l)
                if keep is not None:
                    merged = merged * keep
                    for t in range(2):
                        kept = fields[f, t, rows8(r), :] * keep
                        fields[f, t, rows8(r), :] = kept
                        if f == 3:
                            put_local(t, r, kept)
                fields[f, 2, rows8(r), :] = merged
                if f == 3:
                    put_local(2, r, merged)
            return carry

        lax.fori_loop(lo, hi, body, 0)

    unpack(0, 3, keep_top)
    unpack(3, 35, None)
    unpack(35, 38, keep_bot)

    reduce_b_start(0)

    def strips(halo):
        return 3 - halo, 35 + halo

    def viscous_pass(halo):
        def body(s, carry):
            r = pl.multiple_of(8 + 8 * s, 8)
            x_e, x_n = diff_x(fields[0, :, rows8(r), :]), diff_x(fields[1, :, rows8(r), :])
            y_e = fields[0, :, rows8(r + 1), :] - fields[0, :, rows8(r - 1), :]
            y_n = fields[1, :, rows8(r + 1), :] - fields[1, :, rows8(r - 1), :]
            pressure = fields[2, :, rows8(r), :]
            total, differ, shear = x_e + y_n, x_e - y_n, y_e + x_n
            values = coefficients(total, differ, shear, pressure)
            for i in range(5):
                coef[i, :, rows8(r), :] = values[i]
            p, n = values[0] * total - 0.5 * pressure, values[1] * differ
            stress[0, :, rows8(r), :] = p + n
            stress[1, :, rows8(r), :] = p - n
            stress[2, :, rows8(r), :] = values[1] * shear
            return carry

        lo, hi = strips(halo)
        lax.fori_loop(lo, hi, body, 0)

    def tangent_pass(k, halo):
        def body(s, carry):
            r = pl.multiple_of(8 + 8 * s, 8)
            x_e, x_n = diff_x(krylov[k, 0, :, rows8(r), :]), diff_x(krylov[k, 1, :, rows8(r), :])
            y_e = krylov[k, 0, :, rows8(r + 1), :] - krylov[k, 0, :, rows8(r - 1), :]
            y_n = krylov[k, 1, :, rows8(r + 1), :] - krylov[k, 1, :, rows8(r - 1), :]
            total, differ, shear = x_e + y_n, x_e - y_n, y_e + x_n
            gs, gf, ge = coef[2, :, rows8(r), :], coef[3, :, rows8(r), :], coef[4, :, rows8(r), :]
            q = gs * total + gf * differ + ge * shear
            m8 = coef[1, :, rows8(r), :]
            p = coef[0, :, rows8(r), :] * total - q * gs
            n = m8 * differ - q * gf
            stress[0, :, rows8(r), :] = p + n
            stress[1, :, rows8(r), :] = p - n
            stress[2, :, rows8(r), :] = m8 * shear - q * ge
            return carry

        lo, hi = strips(halo)
        lax.fori_loop(lo, hi, body, 0)

    def stress_force(r):
        t11, t12 = stress[0, :, rows8(r), :], stress[2, :, rows8(r), :]
        y12 = stress[2, :, rows8(r + 1), :] - stress[2, :, rows8(r - 1), :]
        y22 = stress[1, :, rows8(r + 1), :] - stress[1, :, rows8(r - 1), :]
        half = local[2, :, rows8(r), :]
        return half * (diff_x(t11) + y12), half * (diff_x(t12) + y22)

    def residual_at(r):
        force_e, force_n = stress_force(r)
        mass, turn = local[0, :, rows8(r), :], local[1, :, rows8(r), :]
        a, b = fields[0, :, rows8(r), :], fields[1, :, rows8(r), :]
        r_e = fields[4, :, rows8(r), :] + force_e - (mass * a - turn * b)
        r_n = fields[5, :, rows8(r), :] + force_n - (mass * b + turn * a)
        return r_e, r_n

    def jacobian_at(k, r, mid, rho):
        force_e, force_n = stress_force(r)
        mass, turn = local[0, :, rows8(r), :] - mid, local[1, :, rows8(r), :]
        c, d = krylov[k, 0, :, rows8(r), :], krylov[k, 1, :, rows8(r), :]
        w_e = (mass * c - turn * d) - force_e
        w_n = (mass * d + turn * c) - force_n
        if k > 0:
            w_e = w_e - rho * krylov[k - 1, 0, :, rows8(r), :]
            w_n = w_n - rho * krylov[k - 1, 1, :, rows8(r), :]
        return w_e, w_n

    def vector_pass(make, k, halo):
        stored = k < KRYLOV

        def put(r):
            v_e, v_n = make(r)
            if stored:
                krylov[k, 0, :, rows8(r), :] = v_e
                krylov[k, 1, :, rows8(r), :] = v_n
            return v_e, v_n

        def outer(s, carry):
            put(pl.multiple_of(8 + 8 * s, 8))
            return carry

        def inner(s, accs):
            r = pl.multiple_of(8 + 8 * s, 8)
            v_e, v_n = put(r)
            v_e, v_n = v_e[:2], v_n[:2]
            out = []
            for i in range(k + 1):
                if i < k:
                    u_e = krylov[i, 0, pl.ds(0, 2), rows8(r), :]
                    u_n = krylov[i, 1, pl.ds(0, 2), rows8(r), :]
                else:
                    u_e, u_n = v_e, v_n
                product = u_e * v_e + u_n * v_n
                out.append(accs[i] + (product[0] + product[1]))
            return tuple(out)

        lo, hi = strips(halo)
        if halo:
            lax.fori_loop(lo, 3, outer, 0)
        accs = lax.fori_loop(3, 35, inner, tuple(jnp.zeros((8, 128), F32) for _ in range(k + 1)))
        if halo:
            lax.fori_loop(35, hi, outer, 0)
        return accs

    def dot_index(i, k):
        return k * (k + 1) // 2 + i

    mid = square = None
    for step in range(2):
        viscous_pass(3 - step)
        accs = vector_pass(residual_at, 0, 3 - step)
        put_sum(0, accs[0])
        if step == 0:
            mid, square = basis_of(reduce_end(0), 0)
        rho = [None, 2.0 * square] + [square] * 3
        mid8, rho8 = wide(mid), [None if x is None else wide(x) for x in rho]
        norm0 = accs[0]
        for k in range(KRYLOV):
            tangent_pass(k, ((3, 3, 2, 2, 1), (2, 1, 1, 1, 1))[step][k])
            accs = vector_pass(
                lambda r, k=k: jacobian_at(k, r, mid8, rho8[k]), k + 1, ((3, 2, 2, 2, 0), (1, 1, 1, 1, 0))[step][k]
            )
            for i, acc in enumerate(accs):
                put_sum(dot_index(i, k + 1), acc)
            if step == 0 and k == 0:
                def whole(acc):
                    return jnp.sum(jnp.sum(acc, axis=0, keepdims=True), axis=1, keepdims=True)

                g00, g01, g11 = whole(norm0), whole(accs[0]), whole(accs[1])
                m1 = mid[:, 0:1]
                alpha = (g01 + m1 * g00) / (g11 + 2.0 * m1 * g01 + m1 * m1 * g00 + 1e-12)
                alpha = jnp.broadcast_to(alpha, (8, 128))
                for i, acc in enumerate(estimate_pass(alpha)):
                    put_sum(N_DOTS + i, acc)

        reduce_a_start(1 + step, packed_sums(N_SUMS))
        reduce_b_start(1 + step)
        row = reduce_end(1 + step)
        gram = [[None] * 6 for _ in range(6)]
        for j in range(6):
            for i in range(j + 1):
                gram[i][j] = gram[j][i] = splat(row, dot_index(i, j))
        weights = [wide(x) for x in small_solve(gram, mid, rho)]

        def update(s, carry, step=step, weights=weights):
            r = pl.multiple_of(8 + 8 * s, 8)
            tiles = pl.ds(0, 3 if step == 0 else 2)
            for c in range(2):
                total = fields[c, tiles, rows8(r), :]
                for k in range(KRYLOV):
                    total = total + weights[k] * krylov[k, c, tiles, rows8(r), :]
                fields[c, tiles, rows8(r), :] = total
            return carry

        if step == 0:
            for copy in halo_copies:
                copy.wait_send()
        lo, hi = strips(2 if step == 0 else 0)
        lax.fori_loop(lo, hi, update, 0)
        if step == 0:
            mid, square = basis_of(row, N_DOTS)

    outs = []
    for t in range(2):
        outs.append(
            pltpu.make_async_copy(
                fields.at[pl.ds(0, 2), t, own_rows, :], out_ref.at[:, :, pl.ds(128 * t, 128)], out_sem.at[t]
            )
        )
        outs[-1].start()

    picks = []
    for s in range(8):
        picks.append([])
        for i in range(2):
            for j in range(2):
                hit = (ice_ref[i, j] > 0) & (owner_ref[i, j] * 2 + slot_ref[i, j] == s)
                picks[-1].append(jnp.where(hit, 1.0, 0.0).astype(F32))

    def choose(s, carry):
        src = pl.multiple_of(8 * s, 8)
        for c in range(2):
            blocks = []
            for i in range(2):
                for j in range(2):
                    blocks.append(fields[c, j, rows8(pl.multiple_of(TOP + 128 * i + 8 * s, 8)), :])
            for slot in range(8):
                total = blocks[0] * picks[slot][0]
                for b in range(1, 4):
                    total = total + blocks[b] * picks[slot][b]
                send_blocks[slot // 2, slot % 2, c, rows8(src), :] = total
        return carry

    lax.fori_loop(0, 16, choose, 0)

    held_copies = []
    for i in (2, 1, 3):
        other = lax.rem(lat + i, LAT)
        copy = pltpu.make_async_remote_copy(
            src_ref=send_blocks.at[other], dst_ref=recv_blocks.at[i - 1],
            send_sem=held_send.at[i - 1], recv_sem=held_recv.at[i - 1],
            device_id=(other, lon), device_id_type=MESH,
        )
        copy.start()
        held_copies.append(copy)
    for copy in held_copies:
        copy.wait_recv()

    def collect(s, carry):
        r = pl.multiple_of(8 * s, 8)
        for slot in range(2):
            for c in range(2):
                total = send_blocks[lat, slot, c, rows8(r), :]
                for i in range(3):
                    total = total + recv_blocks[i, slot, c, rows8(r), :]
                held_buf[slot, c, rows8(r), :] = total
        return carry

    lax.fori_loop(0, 16, collect, 0)
    last = pltpu.make_async_copy(held_buf, held_ref.at[:, 0], out_sem.at[2])
    last.start()

    for copy in held_copies:
        copy.wait_send()
    for inst in range(3):
        sent = buf_a.at[inst, pl.ds(0, 7)]
        pltpu.make_async_copy(sent, sent, ar_send.at[inst, 0]).wait()
        sent = buf_b.at[inst, pl.ds(0, 15)]
        pltpu.make_async_copy(sent, sent, ar_send.at[inst, 1]).wait()
    for copy in outs:
        copy.wait()
    last.wait()


def on_device(velocity_old, wind_stress, strength, ice_mass, ice_mask, block_owner, block_slot):
    smem = pl.BlockSpec(memory_space=pltpu.SMEM)
    hbm = pl.BlockSpec(memory_space=pl.ANY)
    field = (3, ROWS, 128)
    velocity, held = pl.pallas_call(
        kernel,
        out_shape=(
            jax.ShapeDtypeStruct((2, 256, 256), F32),
            jax.ShapeDtypeStruct((2, 1, 2, 128, 128), F32),
        ),
        in_specs=[smem] * 3 + [hbm] * 4,
        out_specs=(hbm, hbm),
        scratch_shapes=[
            pltpu.VMEM((2, 2, 256, 128), F32),
            pltpu.VMEM((2, 2, 256, 128), F32),
            pltpu.VMEM((2, 256, 128), F32),
            pltpu.VMEM((2, 256, 128), F32),
            pltpu.VMEM((6,) + field, F32),
            pltpu.VMEM((3,) + field, F32),
            pltpu.VMEM((5,) + field, F32),
            pltpu.VMEM((3,) + field, F32),
            pltpu.VMEM((KRYLOV, 2) + field, F32),
            pltpu.VMEM((256, 128), F32),
            pltpu.VMEM((256, 128), F32),
            pltpu.VMEM((ROWS, 128), F32),
            pltpu.VMEM((ROWS, 128), F32),
            pltpu.VMEM((N_SUMS, 128), F32),
            pltpu.VMEM((3, 8, 1, 128), F32),
            pltpu.VMEM((3, 16, 1, 128), F32),
            pltpu.VMEM((4, 2, 2, 128, 128), F32),
            pltpu.VMEM((3, 2, 2, 128, 128), F32),
            pltpu.VMEM((2, 2, 128, 128), F32),
            pltpu.SemaphoreType.DMA((8,)),
            pltpu.SemaphoreType.DMA((8,)),
            pltpu.SemaphoreType.DMA((8,)),
            pltpu.SemaphoreType.DMA((3, 2)),
            pltpu.SemaphoreType.DMA((3, 2)),
            pltpu.SemaphoreType.DMA((3,)),
            pltpu.SemaphoreType.DMA((3,)),
            pltpu.SemaphoreType.DMA((3,)),
        ],
        compiler_params=pltpu.CompilerParams(
            collective_id=0, has_side_effects=True, vmem_limit_bytes=56 * 1024 * 1024
        ),
    )(ice_mask, block_owner, block_slot, velocity_old, wind_stress, strength, ice_mass)
    return velocity, held


def solution(mesh):
    return jax.shard_map(
        on_device,
        mesh=mesh,
        in_specs=(
            P(None, "lat", "lon"),
            P(None, "lat", "lon"),
            P("lat", "lon"),
            P("lat", "lon"),
            P("lat", "lon"),
            P("lat", "lon"),
            P("lat", "lon"),
        ),
        out_specs=(P(None, "lat", "lon"), P("lat", "lon", None, None, None)),
        check_vma=False,
    )
```

```python
import functools

import jax
import jax.numpy as jnp
from jax import lax
from jax.experimental import pallas as pl
from jax.experimental.pallas import tpu as pltpu
from jax.sharding import PartitionSpec as P

MESH = pl.DeviceIdType.MESH
F32 = jnp.float32

KRYLOV = 5
TINY_SQ = 1e-6
LAT = 4
LON = 32

ROWS = 320
TOP = 32
BOT = 288
HALO = 24
OWN_STRIPS = 32

WIDTHS = (22, 22, 22, 20, 20, 20)
OFFSETS = (0, 22, 44, 66, 86, 106)

VISC = 4
TAN = 8
VEC = 8
UPD = 4

N_DOTS = 21
N_SUMS = 24


def lanes(shape):
    return lax.broadcasted_iota(jnp.int32, shape, len(shape) - 1)


def sweep(lo, hi, body, carry, strips):
    count, rest = divmod(hi - lo, strips)

    def step(i, carry):
        return body(pl.multiple_of(8 + 8 * lo + 8 * strips * i, 8), 8 * strips, carry)

    if count:
        carry = lax.fori_loop(0, count, step, carry)
    if rest:
        carry = body(8 + 8 * (hi - rest), 8 * rest, carry)
    return carry


def fold(x):
    x = x.reshape(-1, 8, 128)
    total = x[0]
    for i in range(1, x.shape[0]):
        total = total + x[i]
    return total


def rows8(start):
    return pl.ds(start, 8)


def diff_x(f):
    lane = lanes((1,) + f.shape[1:])
    right = pltpu.roll(f, 127, 2)
    left = pltpu.roll(f, 1, 2)
    right_next = jnp.concatenate([right[1:], right[:1]], axis=0)
    left_next = jnp.concatenate([left[2:], left[:2]], axis=0)
    return jnp.where(lane == 127, right_next, right) - jnp.where(lane == 0, left_next, left)


def diff_x_rough(f):
    return pltpu.roll(f, 127, 2) - pltpu.roll(f, 1, 2)


def coefficients(sum_rate, differ, shear, pressure):
    q = 0.25 * (sum_rate * sum_rate) + 0.0625 * (differ * differ + shear * shear)
    inv = lax.rsqrt(q + 0.04)
    bulk = 0.5 * pressure * inv
    weight = inv * jnp.sqrt(0.5 * bulk)
    eighth = 0.125 * weight
    return 0.5 * bulk, 0.125 * bulk, (0.5 * weight) * sum_rate, eighth * differ, eighth * shear


def spectrum_sums(m2, gs, gf, ge, mass, turn):
    diag = mass + 1.5 * m2 - (gs * gs + gf * gf + ge * ge)
    c11 = 2.5 * m2 - 2.0 * (gs + gf) * (gs + gf)
    c22 = 2.5 * m2 - 2.0 * (gs - gf) * (gs - gf)
    c33 = 2.0 * m2 - 8.0 * ge * ge
    spread = diag * diag + turn * turn + 0.0625 * (c11 * c11 + c22 * c22) + 0.03125 * (c33 * c33)
    return diag, spread


def splat(row, index):
    return jnp.broadcast_to(row[:, index : index + 1], (1, 128))


def wide(row):
    return jnp.broadcast_to(row, (8, 128))


def small_solve(gram, mid, rho):
    def dot(u, gv):
        total = None
        for x, y in zip(u, gv):
            if x is not None:
                total = x * y if total is None else total + x * y
        return total

    def times_gram(u, count):
        return [dot(u, [gram[i][j] for j in range(6)]) for i in range(count)]

    def apply(c):
        out = [None] * 6
        for k, x in enumerate(c):
            if x is None:
                continue
            if k < 5:
                terms = [(k + 1, x), (k, mid * x)]
                if k > 0:
                    terms.append((k - 1, rho[k] * x))
                for at, term in terms:
                    out[at] = term if out[at] is None else out[at] + term
        return out

    beta = jnp.sqrt(gram[0][0] + TINY_SQ)
    basis = [[1.0 / beta] + [None] * 5]
    upper = []
    cosines, sines = [], []
    target = [beta]
    for j in range(KRYLOV):
        u = apply(basis[j])
        gu = times_gram(u, j + 2)
        coeffs = [dot(basis[i][: j + 2], gu) for i in range(j + 1)]
        for i in range(j + 1):
            u = [
                x if y is None else x - coeffs[i] * y
                for x, y in zip(u, basis[i])
            ]
        gu = times_gram(u, j + 2)
        square = jnp.maximum(dot(u[: j + 2], gu), 0.0)
        length = jnp.sqrt(square + TINY_SQ)
        inv_length = 1.0 / length
        basis.append([None if x is None else x * inv_length for x in u])
        column = coeffs + [length]
        for i in range(j):
            a, b = column[i], column[i + 1]
            column[i] = cosines[i] * a + sines[i] * b
            column[i + 1] = cosines[i] * b - sines[i] * a
        a, b = column[j], column[j + 1]
        inv_radius = 1.0 / jnp.sqrt(a * a + b * b)
        cosine, sine = a * inv_radius, b * inv_radius
        cosines.append(cosine)
        sines.append(sine)
        column[j] = cosine * a + sine * b
        upper.append(column[: j + 1])
        target.append(-sine * target[j])
        target[j] = cosine * target[j]
    weights = [None] * KRYLOV
    for j in reversed(range(KRYLOV)):
        known = target[j]
        for k in range(j + 1, KRYLOV):
            known = known - upper[k][j] * weights[k]
        weights[j] = known / upper[j][j]
    out = []
    for k in range(KRYLOV):
        total = None
        for j in range(k, KRYLOV):
            term = weights[j] * basis[j][k]
            total = term if total is None else total + term
        out.append(total)
    return out


def kernel(
    ice_ref, owner_ref, slot_ref, vel_ref, wind_ref, strength_ref, mass_ref,
    out_ref, held_ref,
    st_vel, st_wind, st_strength, st_mass,
    fields, local, coef, stress, krylov,
    pack_e, pack_w, got_l, got_r, sums,
    buf_a, buf_b, send_blocks, recv_blocks, held_buf,
    in_sem, halo_send, halo_recv, ar_send, ar_recv, held_send, held_recv, out_sem,
):
    lat, lon = lax.axis_index("lat"), lax.axis_index("lon")
    north, south = lax.rem(lat + LAT - 1, LAT), lax.rem(lat + 1, LAT)
    east, west = lax.rem(lon + 1, LON), lax.rem(lon + LON - 1, LON)
    core = lax.rem(lon, 2)
    chip = lon // 2
    rank_a = lat * 2 + core
    rank_b = chip

    peers_a = []
    for i in (4, 5, 2, 3, 6, 7, 1):
        other = lax.rem(rank_a + i, 8)
        peers_a.append((other // 2, chip * 2 + lax.rem(other, 2)))
    peers_b = []
    for i in (10, 9, 11, 6, 8, 2, 14, 7, 5, 13, 1, 3, 15, 4, 12):
        peers_b.append((lat, lax.rem(rank_b + i, 16) * 2 + core))
    halo_peers = [(lat, east), (lat, west), (north, east), (north, west), (south, east), (south, west)]

    barrier = pltpu.get_barrier_semaphore()
    greeted = peers_b + peers_a + halo_peers
    for peer in greeted:
        pl.semaphore_signal(barrier, inc=1, device_id=peer, device_id_type=MESH)

    loads = []
    for t in range(2):
        cols = pl.ds(128 * t, 128)
        loads.append(pltpu.make_async_copy(vel_ref.at[:, :, cols], st_vel.at[:, t], in_sem.at[t]))
        loads.append(pltpu.make_async_copy(wind_ref.at[:, :, cols], st_wind.at[:, t], in_sem.at[2 + t]))
        loads.append(pltpu.make_async_copy(strength_ref.at[:, cols], st_strength.at[t], in_sem.at[4 + t]))
        loads.append(pltpu.make_async_copy(mass_ref.at[:, cols], st_mass.at[t], in_sem.at[6 + t]))
    for copy in loads:
        copy.start()
    for copy in loads:
        copy.wait()

    lane8 = lanes((8, 128))
    ice = [[ice_ref[i, j].astype(F32) for j in range(2)] for i in range(2)]
    for half in range(2):

        def prepare(s, carry, half=half):
            src = pl.multiple_of(8 * s, 8)
            dst = pl.multiple_of(TOP + 8 * s, 8)
            for t in range(2):
                w = ice[half][t]
                mass = st_mass[t, rows8(src), :] * w
                v_e = st_vel[0, t, rows8(src), :]
                v_n = st_vel[1, t, rows8(src), :]
                values = (
                    v_e * w,
                    v_n * w,
                    st_strength[t, rows8(src), :] * w,
                    mass,
                    mass * v_e + w * st_wind[0, t, rows8(src), :],
                    mass * v_n + w * st_wind[1, t, rows8(src), :],
                )
                for f in range(6):
                    fields[f, t, rows8(dst), :] = values[f]
                local[0, t, rows8(dst), :] = mass + 0.5 * w
                local[1, t, rows8(dst), :] = 0.3 * mass
                local[2, t, rows8(dst), :] = jnp.zeros((8, 128), F32) + 0.5 * w
                packed = None
                for f in range(6):
                    turn = (OFFSETS[f] if t == 0 else OFFSETS[f] + WIDTHS[f]) % 128
                    rolled = values[f] if turn == 0 else pltpu.roll(values[f], turn, 1)
                    packed = rolled if f == 0 else jnp.where(lane8 >= OFFSETS[f], rolled, packed)
                (pack_w if t == 0 else pack_e)[rows8(src), :] = packed
            return carry

        lax.fori_loop(16 * half, 16 * half + 16, prepare, 0)

    pl.semaphore_wait(barrier, len(greeted))

    own_top, own_bot = pl.ds(TOP, HALO), pl.ds(BOT - HALO, HALO)
    halo_top, halo_bot = pl.ds(TOP - HALO, HALO), pl.ds(BOT, HALO)
    own_rows = pl.ds(TOP, 256)
    src_top, src_bot = pl.ds(0, HALO), pl.ds(256 - HALO, HALO)
    plan = [
        (fields.at[:, pl.ds(0, 2), own_top, :], fields.at[:, pl.ds(0, 2), halo_bot, :], (north, lon)),
        (fields.at[:, pl.ds(0, 2), own_bot, :], fields.at[:, pl.ds(0, 2), halo_top, :], (south, lon)),
        (pack_e.at[src_top, :], got_l.at[halo_bot, :], (north, east)),
        (pack_w.at[src_top, :], got_r.at[halo_bot, :], (north, west)),
        (pack_e.at[src_bot, :], got_l.at[halo_top, :], (south, east)),
        (pack_w.at[src_bot, :], got_r.at[halo_top, :], (south, west)),
        (pack_e, got_l.at[own_rows, :], (lat, east)),
        (pack_w, got_r.at[own_rows, :], (lat, west)),
    ]
    halo_copies = []
    for i, (src, dst, peer) in enumerate(plan):
        copy = pltpu.make_async_remote_copy(
            src_ref=src, dst_ref=dst, send_sem=halo_send.at[i], recv_sem=halo_recv.at[i],
            device_id=peer, device_id_type=MESH,
        )
        copy.start()
        halo_copies.append(copy)

    def reduce_a_start(inst, row):
        buf_a[inst, rank_a] = row
        for peer in peers_a:
            pltpu.make_async_remote_copy(
                src_ref=buf_a.at[inst, rank_a], dst_ref=buf_a.at[inst, rank_a],
                send_sem=ar_send.at[inst, 0], recv_sem=ar_recv.at[inst, 0],
                device_id=peer, device_id_type=MESH,
            ).start()

    def reduce_b_start(inst):
        waited = buf_a.at[inst, pl.ds(0, 7)]
        pltpu.make_async_copy(waited, waited, ar_recv.at[inst, 0]).wait()
        row = buf_a[inst, 0]
        for i in range(1, 8):
            row = row + buf_a[inst, i]
        buf_b[inst, rank_b] = row
        for peer in peers_b:
            pltpu.make_async_remote_copy(
                src_ref=buf_b.at[inst, rank_b], dst_ref=buf_b.at[inst, rank_b],
                send_sem=ar_send.at[inst, 1], recv_sem=ar_recv.at[inst, 1],
                device_id=peer, device_id_type=MESH,
            ).start()

    def reduce_end(inst):
        waited = buf_b.at[inst, pl.ds(0, 15)]
        pltpu.make_async_copy(waited, waited, ar_recv.at[inst, 1]).wait()
        parts = [buf_b[inst, i] for i in range(16)]
        while len(parts) > 1:
            parts = [x + y for x, y in zip(parts[::2], parts[1::2])]
        return parts[0]

    def put_sum(index, acc):
        sums[index : index + 1, :] = jnp.sum(acc, axis=0, keepdims=True)

    def packed_sums(count):
        m = sums[0:count, :]
        total = jnp.sum(m, axis=1, keepdims=True)
        sub = lax.broadcasted_iota(jnp.int32, (count, 128), 0)
        spread = jnp.where(lanes((count, 128)) == sub, total, 0.0)
        return jnp.sum(spread, axis=0, keepdims=True)

    def estimate_pass(alpha):
        both = pl.ds(0, 2)

        def at(c, r):
            flow = fields[c, both, rows8(r), :]
            return flow if alpha is None else flow + alpha * krylov[0, c, both, rows8(r), :]

        def body(i, carry):
            diag_acc, spread_acc, ice_acc = carry
            r = pl.multiple_of(TOP + 8 + 16 * i, 8)
            x_e, x_n = diff_x_rough(at(0, r)), diff_x_rough(at(1, r))
            y_e, y_n = at(0, r + 1) - at(0, r - 1), at(1, r + 1) - at(1, r - 1)
            m2, _, gs, gf, ge = coefficients(x_e + y_n, x_e - y_n, y_e + x_n, fields[2, both, rows8(r), :])
            diag, spread = spectrum_sums(
                m2, gs, gf, ge, local[0, both, rows8(r), :], local[1, both, rows8(r), :]
            )
            weight = local[2, both, rows8(r), :]
            return (
                diag_acc + (diag[0] + diag[1]),
                spread_acc + (spread[0] + spread[1]),
                ice_acc + 2.0 * (weight[0] + weight[1]),
            )

        zero = jnp.zeros((8, 128), F32)
        return lax.fori_loop(0, 15, body, (zero, zero, zero))

    def basis_of(row, at):
        diag, spread, count = splat(row, at), splat(row, at + 1), splat(row, at + 2)
        inv = 1.0 / jnp.maximum(count, 1.0)
        mid = diag * inv
        return mid, jnp.maximum(spread * inv - mid * mid, 0.01)

    for i, acc in enumerate(estimate_pass(None)):
        put_sum(i, acc)
    reduce_a_start(0, packed_sums(8))

    for copy in halo_copies:
        copy.wait_recv()

    keep_top = jnp.where(lat == 0, 0.0, 1.0).astype(F32)
    keep_bot = jnp.where(lat == LAT - 1, 0.0, 1.0).astype(F32)

    def put_local(t, r, mass):
        w = jnp.where(mass > 0.0, 1.0, 0.0)
        local[0, t, rows8(r), :] = mass + 0.5 * w
        local[1, t, rows8(r), :] = 0.3 * mass
        local[2, t, rows8(r), :] = 0.5 * w

    def unpack(lo, hi, keep):
        def body(s, carry):
            r = pl.multiple_of(8 + 8 * s, 8)
            left, right = got_l[rows8(r), :], got_r[rows8(r), :]
            for f in range(6):
                turn_l = (128 - OFFSETS[f] - WIDTHS[f]) % 128
                turn_r = (128 - OFFSETS[f]) % 128
                from_l = left if turn_l == 0 else pltpu.roll(left, turn_l, 1)
                from_r = right if turn_r == 0 else pltpu.roll(right, turn_r, 1)
                merged = jnp.where(lane8 < 64, from_r, from_l)
                if keep is not None:
                    merged = merged * keep
                    for t in range(2):
                        kept = fields[f, t, rows8(r), :] * keep
                        fields[f, t, rows8(r), :] = kept
                        if f == 3:
                            put_local(t, r, kept)
                fields[f, 2, rows8(r), :] = merged
                if f == 3:
                    put_local(2, r, merged)
            return carry

        lax.fori_loop(lo, hi, body, 0)

    unpack(0, 3, keep_top)
    unpack(3, 35, None)
    unpack(35, 38, keep_bot)

    reduce_b_start(0)

    def strips(halo):
        return 3 - halo, 35 + halo

    def viscous_pass(halo):
        def body(r, n, carry):
            here, up, down = pl.ds(r, n), pl.ds(r + 1, n), pl.ds(r - 1, n)
            x_e, x_n = diff_x(fields[0, :, here, :]), diff_x(fields[1, :, here, :])
            y_e = fields[0, :, up, :] - fields[0, :, down, :]
            y_n = fields[1, :, up, :] - fields[1, :, down, :]
            pressure = fields[2, :, here, :]
            total, differ, shear = x_e + y_n, x_e - y_n, y_e + x_n
            values = coefficients(total, differ, shear, pressure)
            for i in range(5):
                coef[i, :, here, :] = values[i]
            p, n = values[0] * total - 0.5 * pressure, values[1] * differ
            stress[0, :, here, :] = p + n
            stress[1, :, here, :] = p - n
            stress[2, :, here, :] = values[1] * shear
            return carry

        lo, hi = strips(halo)
        sweep(lo, hi, body, 0, VISC)

    def tangent_pass(k, halo):
        def body(r, n, carry):
            here, up, down = pl.ds(r, n), pl.ds(r + 1, n), pl.ds(r - 1, n)
            x_e, x_n = diff_x(krylov[k, 0, :, here, :]), diff_x(krylov[k, 1, :, here, :])
            y_e = krylov[k, 0, :, up, :] - krylov[k, 0, :, down, :]
            y_n = krylov[k, 1, :, up, :] - krylov[k, 1, :, down, :]
            total, differ, shear = x_e + y_n, x_e - y_n, y_e + x_n
            gs, gf, ge = coef[2, :, here, :], coef[3, :, here, :], coef[4, :, here, :]
            q = gs * total + gf * differ + ge * shear
            m8 = coef[1, :, here, :]
            p = coef[0, :, here, :] * total - q * gs
            n = m8 * differ - q * gf
            stress[0, :, here, :] = p + n
            stress[1, :, here, :] = p - n
            stress[2, :, here, :] = m8 * shear - q * ge
            return carry

        lo, hi = strips(halo)
        sweep(lo, hi, body, 0, TAN)

    def stress_force(r, n):
        here, up, down = pl.ds(r, n), pl.ds(r + 1, n), pl.ds(r - 1, n)
        t11, t12 = stress[0, :, here, :], stress[2, :, here, :]
        y12 = stress[2, :, up, :] - stress[2, :, down, :]
        y22 = stress[1, :, up, :] - stress[1, :, down, :]
        half = local[2, :, here, :]
        return half * (diff_x(t11) + y12), half * (diff_x(t12) + y22)

    def residual_at(r, n):
        here = pl.ds(r, n)
        force_e, force_n = stress_force(r, n)
        mass, turn = local[0, :, here, :], local[1, :, here, :]
        a, b = fields[0, :, here, :], fields[1, :, here, :]
        r_e = fields[4, :, here, :] + force_e - (mass * a - turn * b)
        r_n = fields[5, :, here, :] + force_n - (mass * b + turn * a)
        return r_e, r_n

    def jacobian_at(k, r, n, mid, rho):
        here = pl.ds(r, n)
        force_e, force_n = stress_force(r, n)
        mass, turn = local[0, :, here, :] - mid, local[1, :, here, :]
        c, d = krylov[k, 0, :, here, :], krylov[k, 1, :, here, :]
        w_e = (mass * c - turn * d) - force_e
        w_n = (mass * d + turn * c) - force_n
        if k > 0:
            w_e = w_e - rho * krylov[k - 1, 0, :, here, :]
            w_n = w_n - rho * krylov[k - 1, 1, :, here, :]
        return w_e, w_n

    def vector_pass(make, k, halo):
        stored = k < KRYLOV

        def put(r, n):
            v_e, v_n = make(r, n)
            if stored:
                krylov[k, 0, :, pl.ds(r, n), :] = v_e
                krylov[k, 1, :, pl.ds(r, n), :] = v_n
            return v_e, v_n

        def outer(r, n, carry):
            put(r, n)
            return carry

        def inner(r, n, accs):
            v_e, v_n = put(r, n)
            v_e, v_n = v_e[:2], v_n[:2]
            out = []
            for i in range(k + 1):
                if i < k:
                    u_e = krylov[i, 0, pl.ds(0, 2), pl.ds(r, n), :]
                    u_n = krylov[i, 1, pl.ds(0, 2), pl.ds(r, n), :]
                else:
                    u_e, u_n = v_e, v_n
                out.append(accs[i] + fold(u_e * v_e + u_n * v_n))
            return tuple(out)

        lo, hi = strips(halo)
        if halo:
            sweep(lo, 3, outer, 0, halo)
        accs = sweep(3, 35, inner, tuple(jnp.zeros((8, 128), F32) for _ in range(k + 1)), VEC)
        if halo:
            sweep(35, hi, outer, 0, halo)
        return accs

    def dot_index(i, k):
        return k * (k + 1) // 2 + i

    mid = square = None
    for step in range(2):
        viscous_pass(3 - step)
        accs = vector_pass(residual_at, 0, 3 - step)
        put_sum(0, accs[0])
        if step == 0:
            mid, square = basis_of(reduce_end(0), 0)
        rho = [None, 2.0 * square] + [square] * 3
        mid8, rho8 = mid, rho
        norm0 = accs[0]
        for k in range(KRYLOV):
            tangent_pass(k, ((3, 3, 2, 2, 1), (2, 1, 1, 1, 1))[step][k])
            accs = vector_pass(
                lambda r, n, k=k: jacobian_at(k, r, n, mid8, rho8[k]), k + 1, ((3, 2, 2, 2, 0), (1, 1, 1, 1, 0))[step][k]
            )
            for i, acc in enumerate(accs):
                put_sum(dot_index(i, k + 1), acc)
            if step == 0 and k == 0:
                def whole(acc):
                    return jnp.sum(jnp.sum(acc, axis=0, keepdims=True), axis=1, keepdims=True)

                g00, g01, g11 = whole(norm0), whole(accs[0]), whole(accs[1])
                m1 = mid[:, 0:1]
                alpha = (g01 + m1 * g00) / (g11 + 2.0 * m1 * g01 + m1 * m1 * g00 + 1e-12)
                alpha = jnp.broadcast_to(alpha, (8, 128))
                for i, acc in enumerate(estimate_pass(alpha)):
                    put_sum(N_DOTS + i, acc)

        reduce_a_start(1 + step, packed_sums(N_SUMS))
        reduce_b_start(1 + step)
        row = reduce_end(1 + step)
        gram = [[None] * 6 for _ in range(6)]
        for j in range(6):
            for i in range(j + 1):
                gram[i][j] = gram[j][i] = splat(row, dot_index(i, j))
        weights = small_solve(gram, mid, rho)

        def update(r, n, carry, step=step, weights=weights):
            tiles = pl.ds(0, 3 if step == 0 else 2)
            for c in range(2):
                total = fields[c, tiles, pl.ds(r, n), :]
                for k in range(KRYLOV):
                    total = total + weights[k] * krylov[k, c, tiles, pl.ds(r, n), :]
                fields[c, tiles, pl.ds(r, n), :] = total
            return carry

        if step == 0:
            for copy in halo_copies:
                copy.wait_send()
        lo, hi = strips(2 if step == 0 else 0)
        sweep(lo, hi, update, 0, UPD)
        if step == 0:
            mid, square = basis_of(row, N_DOTS)

    outs = []
    for t in range(2):
        outs.append(
            pltpu.make_async_copy(
                fields.at[pl.ds(0, 2), t, own_rows, :], out_ref.at[:, :, pl.ds(128 * t, 128)], out_sem.at[t]
            )
        )
        outs[-1].start()

    picks = []
    for s in range(8):
        picks.append([])
        for i in range(2):
            for j in range(2):
                hit = (ice_ref[i, j] > 0) & (owner_ref[i, j] * 2 + slot_ref[i, j] == s)
                picks[-1].append(jnp.where(hit, 1.0, 0.0).astype(F32))

    def choose(s, carry):
        src = pl.multiple_of(8 * s, 8)
        for c in range(2):
            blocks = []
            for i in range(2):
                for j in range(2):
                    blocks.append(fields[c, j, rows8(pl.multiple_of(TOP + 128 * i + 8 * s, 8)), :])
            for slot in range(8):
                total = blocks[0] * picks[slot][0]
                for b in range(1, 4):
                    total = total + blocks[b] * picks[slot][b]
                send_blocks[slot // 2, slot % 2, c, rows8(src), :] = total
        return carry

    lax.fori_loop(0, 16, choose, 0)

    held_copies = []
    for i in (2, 1, 3):
        other = lax.rem(lat + i, LAT)
        copy = pltpu.make_async_remote_copy(
            src_ref=send_blocks.at[other], dst_ref=recv_blocks.at[i - 1],
            send_sem=held_send.at[i - 1], recv_sem=held_recv.at[i - 1],
            device_id=(other, lon), device_id_type=MESH,
        )
        copy.start()
        held_copies.append(copy)
    for copy in held_copies:
        copy.wait_recv()

    def collect(s, carry):
        r = pl.multiple_of(8 * s, 8)
        for slot in range(2):
            for c in range(2):
                total = send_blocks[lat, slot, c, rows8(r), :]
                for i in range(3):
                    total = total + recv_blocks[i, slot, c, rows8(r), :]
                held_buf[slot, c, rows8(r), :] = total
        return carry

    lax.fori_loop(0, 16, collect, 0)
    last = pltpu.make_async_copy(held_buf, held_ref.at[:, 0], out_sem.at[2])
    last.start()

    for copy in held_copies:
        copy.wait_send()
    for inst in range(3):
        sent = buf_a.at[inst, pl.ds(0, 7)]
        pltpu.make_async_copy(sent, sent, ar_send.at[inst, 0]).wait()
        sent = buf_b.at[inst, pl.ds(0, 15)]
        pltpu.make_async_copy(sent, sent, ar_send.at[inst, 1]).wait()
    for copy in outs:
        copy.wait()
    last.wait()


def on_device(velocity_old, wind_stress, strength, ice_mass, ice_mask, block_owner, block_slot):
    smem = pl.BlockSpec(memory_space=pltpu.SMEM)
    hbm = pl.BlockSpec(memory_space=pl.ANY)
    field = (3, ROWS, 128)
    velocity, held = pl.pallas_call(
        kernel,
        out_shape=(
            jax.ShapeDtypeStruct((2, 256, 256), F32),
            jax.ShapeDtypeStruct((2, 1, 2, 128, 128), F32),
        ),
        in_specs=[smem] * 3 + [hbm] * 4,
        out_specs=(hbm, hbm),
        scratch_shapes=[
            pltpu.VMEM((2, 2, 256, 128), F32),
            pltpu.VMEM((2, 2, 256, 128), F32),
            pltpu.VMEM((2, 256, 128), F32),
            pltpu.VMEM((2, 256, 128), F32),
            pltpu.VMEM((6,) + field, F32),
            pltpu.VMEM((3,) + field, F32),
            pltpu.VMEM((5,) + field, F32),
            pltpu.VMEM((3,) + field, F32),
            pltpu.VMEM((KRYLOV, 2) + field, F32),
            pltpu.VMEM((256, 128), F32),
            pltpu.VMEM((256, 128), F32),
            pltpu.VMEM((ROWS, 128), F32),
            pltpu.VMEM((ROWS, 128), F32),
            pltpu.VMEM((N_SUMS, 128), F32),
            pltpu.VMEM((3, 8, 1, 128), F32),
            pltpu.VMEM((3, 16, 1, 128), F32),
            pltpu.VMEM((4, 2, 2, 128, 128), F32),
            pltpu.VMEM((3, 2, 2, 128, 128), F32),
            pltpu.VMEM((2, 2, 128, 128), F32),
            pltpu.SemaphoreType.DMA((8,)),
            pltpu.SemaphoreType.DMA((8,)),
            pltpu.SemaphoreType.DMA((8,)),
            pltpu.SemaphoreType.DMA((3, 2)),
            pltpu.SemaphoreType.DMA((3, 2)),
            pltpu.SemaphoreType.DMA((3,)),
            pltpu.SemaphoreType.DMA((3,)),
            pltpu.SemaphoreType.DMA((3,)),
        ],
        compiler_params=pltpu.CompilerParams(
            collective_id=0, has_side_effects=True, vmem_limit_bytes=56 * 1024 * 1024
        ),
    )(ice_mask, block_owner, block_slot, velocity_old, wind_stress, strength, ice_mass)
    return velocity, held


def solution(mesh):
    return jax.shard_map(
        on_device,
        mesh=mesh,
        in_specs=(
            P(None, "lat", "lon"),
            P(None, "lat", "lon"),
            P("lat", "lon"),
            P("lat", "lon"),
            P("lat", "lon"),
            P("lat", "lon"),
            P("lat", "lon"),
        ),
        out_specs=(P(None, "lat", "lon"), P("lat", "lon", None, None, None)),
        check_vma=False,
    )
```

```python
import functools

import jax
import jax.numpy as jnp
from jax import lax
from jax.experimental import pallas as pl
from jax.experimental.pallas import tpu as pltpu
from jax.sharding import PartitionSpec as P

MESH = pl.DeviceIdType.MESH
F32 = jnp.float32

KRYLOV = 5
TINY_SQ = 1e-6
LAT = 4
LON = 32

ROWS = 320
TOP = 32
BOT = 288
HALO = 24
OWN_STRIPS = 32

WIDTHS = (22, 22, 22, 20, 20, 20)
OFFSETS = (0, 22, 44, 66, 86, 106)

VISC = 4
TAN = 19
VEC = 8
UPD = 4

N_DOTS = 21
N_SUMS = 24


def lanes(shape):
    return lax.broadcasted_iota(jnp.int32, shape, len(shape) - 1)


def sweep(lo, hi, body, carry, strips):
    count, rest = divmod(hi - lo, strips)

    def step(i, carry):
        return body(pl.multiple_of(8 + 8 * lo + 8 * strips * i, 8), 8 * strips, carry)

    if count:
        carry = lax.fori_loop(0, count, step, carry)
    if rest:
        carry = body(8 + 8 * (hi - rest), 8 * rest, carry)
    return carry


def fold(x):
    x = x.reshape(-1, 8, 128)
    total = x[0]
    for i in range(1, x.shape[0]):
        total = total + x[i]
    return total


def rows8(start):
    return pl.ds(start, 8)


def diff_x(f):
    lane = lanes((1,) + f.shape[1:])
    right = pltpu.roll(f, 127, 2)
    left = pltpu.roll(f, 1, 2)
    right_next = jnp.concatenate([right[1:], right[:1]], axis=0)
    left_next = jnp.concatenate([left[2:], left[:2]], axis=0)
    return jnp.where(lane == 127, right_next, right) - jnp.where(lane == 0, left_next, left)


def diff_x_rough(f):
    return pltpu.roll(f, 127, 2) - pltpu.roll(f, 1, 2)


def coefficients(sum_rate, differ, shear, pressure):
    q = 0.25 * (sum_rate * sum_rate) + 0.0625 * (differ * differ + shear * shear)
    inv = lax.rsqrt(q + 0.04)
    bulk = 0.5 * pressure * inv
    weight = inv * jnp.sqrt(0.5 * bulk)
    eighth = 0.125 * weight
    return 0.5 * bulk, 0.125 * bulk, (0.5 * weight) * sum_rate, eighth * differ, eighth * shear


def spectrum_sums(m2, gs, gf, ge, mass, turn):
    diag = mass + 1.5 * m2 - (gs * gs + gf * gf + ge * ge)
    c11 = 2.5 * m2 - 2.0 * (gs + gf) * (gs + gf)
    c22 = 2.5 * m2 - 2.0 * (gs - gf) * (gs - gf)
    c33 = 2.0 * m2 - 8.0 * ge * ge
    spread = diag * diag + turn * turn + 0.0625 * (c11 * c11 + c22 * c22) + 0.03125 * (c33 * c33)
    return diag, spread


def splat(row, index):
    return jnp.broadcast_to(row[:, index : index + 1], (1, 128))


def wide(row):
    return jnp.broadcast_to(row, (8, 128))


def small_solve(gram, mid, rho):
    def dot(u, gv):
        total = None
        for x, y in zip(u, gv):
            if x is not None:
                total = x * y if total is None else total + x * y
        return total

    def times_gram(u, count):
        return [dot(u, [gram[i][j] for j in range(6)]) for i in range(count)]

    def apply(c):
        out = [None] * 6
        for k, x in enumerate(c):
            if x is None:
                continue
            if k < 5:
                terms = [(k + 1, x), (k, mid * x)]
                if k > 0:
                    terms.append((k - 1, rho[k] * x))
                for at, term in terms:
                    out[at] = term if out[at] is None else out[at] + term
        return out

    beta = jnp.sqrt(gram[0][0] + TINY_SQ)
    basis = [[1.0 / beta] + [None] * 5]
    upper = []
    cosines, sines = [], []
    target = [beta]
    for j in range(KRYLOV):
        u = apply(basis[j])
        gu = times_gram(u, j + 2)
        coeffs = [dot(basis[i][: j + 2], gu) for i in range(j + 1)]
        for i in range(j + 1):
            u = [
                x if y is None else x - coeffs[i] * y
                for x, y in zip(u, basis[i])
            ]
        gu = times_gram(u, j + 2)
        square = jnp.maximum(dot(u[: j + 2], gu), 0.0)
        length = jnp.sqrt(square + TINY_SQ)
        inv_length = 1.0 / length
        basis.append([None if x is None else x * inv_length for x in u])
        column = coeffs + [length]
        for i in range(j):
            a, b = column[i], column[i + 1]
            column[i] = cosines[i] * a + sines[i] * b
            column[i + 1] = cosines[i] * b - sines[i] * a
        a, b = column[j], column[j + 1]
        inv_radius = 1.0 / jnp.sqrt(a * a + b * b)
        cosine, sine = a * inv_radius, b * inv_radius
        cosines.append(cosine)
        sines.append(sine)
        column[j] = cosine * a + sine * b
        upper.append(column[: j + 1])
        target.append(-sine * target[j])
        target[j] = cosine * target[j]
    weights = [None] * KRYLOV
    for j in reversed(range(KRYLOV)):
        known = target[j]
        for k in range(j + 1, KRYLOV):
            known = known - upper[k][j] * weights[k]
        weights[j] = known / upper[j][j]
    out = []
    for k in range(KRYLOV):
        total = None
        for j in range(k, KRYLOV):
            term = weights[j] * basis[j][k]
            total = term if total is None else total + term
        out.append(total)
    return out


def kernel(
    ice_ref, owner_ref, slot_ref, vel_ref, wind_ref, strength_ref, mass_ref,
    out_ref, held_ref,
    st_vel, st_wind, st_strength, st_mass,
    fields, local, coef, stress, krylov,
    pack_e, pack_w, got_l, got_r, sums,
    buf_a, buf_b, send_blocks, recv_blocks, sum_blocks, held_buf,
    in_sem, halo_send, halo_recv, ar_send, ar_recv, held_send, held_recv, out_sem,
):
    lat, lon = lax.axis_index("lat"), lax.axis_index("lon")
    north, south = lax.rem(lat + LAT - 1, LAT), lax.rem(lat + 1, LAT)
    east, west = lax.rem(lon + 1, LON), lax.rem(lon + LON - 1, LON)
    core = lax.rem(lon, 2)
    chip = lon // 2
    rank_b = lat * 16 + chip
    y, z = chip // 4, lax.rem(chip, 4)

    partner = (lat, chip * 2 + (1 - core))
    peers_b = []
    shifts = [(i, j, k) for i in range(4) for j in range(4) for k in range(4) if i or j or k]
    for i, j, k in sorted(shifts, key=lambda d: -sum(min(n, 4 - n) + (n > 0) for n in d)):
        other = lax.rem(y + j, 4) * 4 + lax.rem(z + k, 4)
        peers_b.append((lax.rem(lat + i, 4), other * 2 + core))
    halo_peers = [(lat, east), (lat, west), (north, east), (north, west), (south, east), (south, west)]

    loads = []
    for t in range(2):
        cols = pl.ds(128 * t, 128)
        loads.append(pltpu.make_async_copy(vel_ref.at[:, :, cols], st_vel.at[:, t], in_sem.at[t]))
        loads.append(pltpu.make_async_copy(wind_ref.at[:, :, cols], st_wind.at[:, t], in_sem.at[2 + t]))
        loads.append(pltpu.make_async_copy(strength_ref.at[:, cols], st_strength.at[t], in_sem.at[4 + t]))
        loads.append(pltpu.make_async_copy(mass_ref.at[:, cols], st_mass.at[t], in_sem.at[6 + t]))
    for copy in loads:
        copy.start()

    barrier = pltpu.get_barrier_semaphore()
    greeted = peers_b + halo_peers
    for peer in greeted:
        pl.semaphore_signal(barrier, inc=1, device_id=peer, device_id_type=MESH)

    for copy in loads:
        copy.wait()

    ice = [[ice_ref[i, j].astype(F32) for j in range(2)] for i in range(2)]
    for half in range(2):

        def prepare(s, carry, half=half):
            src = pl.ds(pl.multiple_of(32 * s, 32), 32)
            dst = pl.ds(pl.multiple_of(TOP + 32 * s, 32), 32)
            lane = lanes((32, 128))
            for t in range(2):
                w = ice[half][t]
                mass = st_mass[t, src, :] * w
                v_e = st_vel[0, t, src, :]
                v_n = st_vel[1, t, src, :]
                values = (
                    v_e * w,
                    v_n * w,
                    st_strength[t, src, :] * w,
                    mass,
                    mass * v_e + w * st_wind[0, t, src, :],
                    mass * v_n + w * st_wind[1, t, src, :],
                )
                for f in range(6):
                    fields[f, t, dst, :] = values[f]
                local[0, t, dst, :] = mass + 0.5 * w
                local[1, t, dst, :] = 0.3 * mass
                local[2, t, dst, :] = jnp.zeros((32, 128), F32) + 0.5 * w
                packed = None
                for f in range(6):
                    turn = (OFFSETS[f] if t == 0 else OFFSETS[f] + WIDTHS[f]) % 128
                    rolled = values[f] if turn == 0 else pltpu.roll(values[f], turn, 1)
                    packed = rolled if f == 0 else jnp.where(lane >= OFFSETS[f], rolled, packed)
                (pack_w if t == 0 else pack_e)[src, :] = packed
            return carry

        lax.fori_loop(4 * half, 4 * half + 4, prepare, 0)

    first, second, both = pl.ds(0, 3), pl.ds(3, 3), pl.ds(0, 2)
    def reduce_a_start(inst, row):
        buf_a[inst, core] = row
        pltpu.make_async_remote_copy(
            src_ref=buf_a.at[inst, core], dst_ref=buf_a.at[inst, core],
            send_sem=ar_send.at[inst, 0], recv_sem=ar_recv.at[inst, 0],
            device_id=partner, device_id_type=MESH,
        ).start()

    def reduce_b_start(inst):
        waited = buf_a.at[inst, 0]
        pltpu.make_async_copy(waited, waited, ar_recv.at[inst, 0]).wait()
        buf_b[inst, rank_b] = buf_a[inst, 0] + buf_a[inst, 1]
        for peer in peers_b:
            pltpu.make_async_remote_copy(
                src_ref=buf_b.at[inst, rank_b], dst_ref=buf_b.at[inst, rank_b],
                send_sem=ar_send.at[inst, 1], recv_sem=ar_recv.at[inst, 1],
                device_id=peer, device_id_type=MESH,
            ).start()

    def reduce_end(inst):
        waited = buf_b.at[inst, pl.ds(0, 63)]
        pltpu.make_async_copy(waited, waited, ar_recv.at[inst, 1]).wait()
        parts = [buf_b[inst, pl.ds(8 * i, 8)] for i in range(8)]
        while len(parts) > 1:
            parts = [x + y for x, y in zip(parts[::2], parts[1::2])]
        return jnp.sum(parts[0], axis=0)

    def put_sum(index, acc):
        sums[index : index + 1, :] = jnp.sum(acc, axis=0, keepdims=True)

    def packed_sums(count):
        m = sums[0:count, :]
        total = jnp.sum(m, axis=1, keepdims=True)
        sub = lax.broadcasted_iota(jnp.int32, (count, 128), 0)
        spread = jnp.where(lanes((count, 128)) == sub, total, 0.0)
        return jnp.sum(spread, axis=0, keepdims=True)

    def estimate_pass(alpha):
        def at(c, r):
            flow = fields[c, both, rows8(r), :]
            return flow if alpha is None else flow + alpha * krylov[0, c, both, rows8(r), :]

        def one(r, carry):
            diag_acc, spread_acc, ice_acc = carry
            x_e, x_n = diff_x_rough(at(0, r)), diff_x_rough(at(1, r))
            y_e, y_n = at(0, r + 1) - at(0, r - 1), at(1, r + 1) - at(1, r - 1)
            m2, _, gs, gf, ge = coefficients(x_e + y_n, x_e - y_n, y_e + x_n, fields[2, both, rows8(r), :])
            diag, spread = spectrum_sums(
                m2, gs, gf, ge, local[0, both, rows8(r), :], local[1, both, rows8(r), :]
            )
            weight = local[2, both, rows8(r), :]
            return (
                diag_acc + (diag[0] + diag[1]),
                spread_acc + (spread[0] + spread[1]),
                ice_acc + 2.0 * (weight[0] + weight[1]),
            )

        def body(i, carry):
            for j in range(5):
                carry = one(pl.multiple_of(TOP + 8 + 80 * i + 16 * j, 8), carry)
            return carry

        zero = jnp.zeros((8, 128), F32)
        return lax.fori_loop(0, 3, body, (zero, zero, zero))

    def basis_of(row, at):
        diag, spread, count = splat(row, at), splat(row, at + 1), splat(row, at + 2)
        inv = 1.0 / jnp.maximum(count, 1.0)
        mid = diag * inv
        return mid, jnp.maximum(spread * inv - mid * mid, 0.01)

    for i, acc in enumerate(estimate_pass(None)):
        put_sum(i, acc)
    first_sums = packed_sums(8)

    pl.semaphore_wait(barrier, len(greeted))

    own_top, own_bot = pl.ds(TOP, HALO), pl.ds(BOT - HALO, HALO)
    halo_top, halo_bot = pl.ds(TOP - HALO, HALO), pl.ds(BOT, HALO)
    own_rows = pl.ds(TOP, 256)
    src_top, src_bot = pl.ds(0, HALO), pl.ds(256 - HALO, HALO)
    plan = [
        (fields.at[first, both, own_top, :], fields.at[first, both, halo_bot, :], (north, lon)),
        (fields.at[first, both, own_bot, :], fields.at[first, both, halo_top, :], (south, lon)),
        (pack_e.at[src_top, :], got_l.at[halo_bot, :], (north, east)),
        (pack_w.at[src_top, :], got_r.at[halo_bot, :], (north, west)),
        (pack_e.at[src_bot, :], got_l.at[halo_top, :], (south, east)),
        (pack_w.at[src_bot, :], got_r.at[halo_top, :], (south, west)),
        (pack_e, got_l.at[own_rows, :], (lat, east)),
        (pack_w, got_r.at[own_rows, :], (lat, west)),
        (fields.at[second, both, own_top, :], fields.at[second, both, halo_bot, :], (north, lon)),
        (fields.at[second, both, own_bot, :], fields.at[second, both, halo_top, :], (south, lon)),
    ]
    halo_copies = []
    for i, (src, dst, peer) in enumerate(plan):
        copy = pltpu.make_async_remote_copy(
            src_ref=src, dst_ref=dst, send_sem=halo_send.at[i], recv_sem=halo_recv.at[i],
            device_id=peer, device_id_type=MESH,
        )
        copy.start()
        halo_copies.append(copy)

    reduce_a_start(0, first_sums)

    keep_top = jnp.where(lat == 0, 0.0, 1.0).astype(F32)
    keep_bot = jnp.where(lat == LAT - 1, 0.0, 1.0).astype(F32)

    def put_local(t, here, mass):
        w = jnp.where(mass > 0.0, 1.0, 0.0)
        local[0, t, here, :] = mass + 0.5 * w
        local[1, t, here, :] = 0.3 * mass
        local[2, t, here, :] = 0.5 * w

    def unpack(keep):
        def body(r, n, carry):
            here = pl.ds(r, n)
            left, right = got_l[here, :], got_r[here, :]
            lane = lanes((n, 128))
            for f in range(6):
                turn_l = (128 - OFFSETS[f] - WIDTHS[f]) % 128
                turn_r = (128 - OFFSETS[f]) % 128
                from_l = left if turn_l == 0 else pltpu.roll(left, turn_l, 1)
                from_r = right if turn_r == 0 else pltpu.roll(right, turn_r, 1)
                merged = jnp.where(lane < 64, from_r, from_l)
                if keep is not None:
                    merged = merged * keep
                fields[f, 2, here, :] = merged
                if f == 3:
                    put_local(2, here, merged)
            return carry

        return body

    def clear_first(top, keep):
        fields[first, both, pl.ds(top, HALO), :] = fields[first, both, pl.ds(top, HALO), :] * keep

    def clear_second(top, keep):
        here = pl.ds(top, HALO)
        for t in range(2):
            for f in range(3, 6):
                kept = fields[f, t, here, :] * keep
                fields[f, t, here, :] = kept
                if f == 3:
                    put_local(t, here, kept)

    for copy in halo_copies[:8]:
        copy.wait_recv()
    sweep(0, 3, unpack(keep_top), 0, 3)
    sweep(3, 35, unpack(None), 0, 4)
    sweep(35, 38, unpack(keep_bot), 0, 3)
    clear_first(TOP - HALO, keep_top)
    clear_first(BOT, keep_bot)

    reduce_b_start(0)

    def strips(halo):
        return 3 - halo, 35 + halo

    def viscous_pass(halo):
        def body(r, n, carry):
            here, up, down = pl.ds(r, n), pl.ds(r + 1, n), pl.ds(r - 1, n)
            x_e, x_n = diff_x(fields[0, :, here, :]), diff_x(fields[1, :, here, :])
            y_e = fields[0, :, up, :] - fields[0, :, down, :]
            y_n = fields[1, :, up, :] - fields[1, :, down, :]
            pressure = fields[2, :, here, :]
            total, differ, shear = x_e + y_n, x_e - y_n, y_e + x_n
            values = coefficients(total, differ, shear, pressure)
            for i in range(5):
                coef[i, :, here, :] = values[i]
            p, n = values[0] * total - 0.5 * pressure, values[1] * differ
            stress[0, :, here, :] = p + n
            stress[1, :, here, :] = p - n
            stress[2, :, here, :] = values[1] * shear
            return carry

        lo, hi = strips(halo)
        sweep(lo, hi, body, 0, VISC)

    def tangent_pass(k, halo):
        def body(r, n, carry):
            here, up, down = pl.ds(r, n), pl.ds(r + 1, n), pl.ds(r - 1, n)
            x_e, x_n = diff_x(krylov[k, 0, :, here, :]), diff_x(krylov[k, 1, :, here, :])
            y_e = krylov[k, 0, :, up, :] - krylov[k, 0, :, down, :]
            y_n = krylov[k, 1, :, up, :] - krylov[k, 1, :, down, :]
            total, differ, shear = x_e + y_n, x_e - y_n, y_e + x_n
            gs, gf, ge = coef[2, :, here, :], coef[3, :, here, :], coef[4, :, here, :]
            q = gs * total + gf * differ + ge * shear
            m8 = coef[1, :, here, :]
            p = coef[0, :, here, :] * total - q * gs
            n = m8 * differ - q * gf
            stress[0, :, here, :] = p + n
            stress[1, :, here, :] = p - n
            stress[2, :, here, :] = m8 * shear - q * ge
            return carry

        lo, hi = strips(halo)
        sweep(lo, hi, body, 0, TAN)

    def stress_force(r, n):
        here, up, down = pl.ds(r, n), pl.ds(r + 1, n), pl.ds(r - 1, n)
        t11, t12 = stress[0, :, here, :], stress[2, :, here, :]
        y12 = stress[2, :, up, :] - stress[2, :, down, :]
        y22 = stress[1, :, up, :] - stress[1, :, down, :]
        half = local[2, :, here, :]
        return half * (diff_x(t11) + y12), half * (diff_x(t12) + y22)

    def residual_at(r, n):
        here = pl.ds(r, n)
        force_e, force_n = stress_force(r, n)
        mass, turn = local[0, :, here, :], local[1, :, here, :]
        a, b = fields[0, :, here, :], fields[1, :, here, :]
        r_e = fields[4, :, here, :] + force_e - (mass * a - turn * b)
        r_n = fields[5, :, here, :] + force_n - (mass * b + turn * a)
        return r_e, r_n

    def jacobian_at(k, r, n, mid, rho):
        here = pl.ds(r, n)
        force_e, force_n = stress_force(r, n)
        mass, turn = local[0, :, here, :] - mid, local[1, :, here, :]
        c, d = krylov[k, 0, :, here, :], krylov[k, 1, :, here, :]
        w_e = (mass * c - turn * d) - force_e
        w_n = (mass * d + turn * c) - force_n
        if k > 0:
            w_e = w_e - rho * krylov[k - 1, 0, :, here, :]
            w_n = w_n - rho * krylov[k - 1, 1, :, here, :]
        return w_e, w_n

    def vector_pass(make, k, halo):
        stored = k < KRYLOV

        def put(r, n):
            v_e, v_n = make(r, n)
            if stored:
                krylov[k, 0, :, pl.ds(r, n), :] = v_e
                krylov[k, 1, :, pl.ds(r, n), :] = v_n
            return v_e, v_n

        def outer(r, n, carry):
            put(r, n)
            return carry

        def inner(r, n, accs):
            v_e, v_n = put(r, n)
            v_e, v_n = v_e[:2], v_n[:2]
            out = []
            for i in range(k + 1):
                if i < k:
                    u_e = krylov[i, 0, pl.ds(0, 2), pl.ds(r, n), :]
                    u_n = krylov[i, 1, pl.ds(0, 2), pl.ds(r, n), :]
                else:
                    u_e, u_n = v_e, v_n
                out.append(accs[i] + fold(u_e * v_e + u_n * v_n))
            return tuple(out)

        lo, hi = strips(halo)
        if halo:
            sweep(lo, 3, outer, 0, halo)
        accs = sweep(3, 35, inner, tuple(jnp.zeros((8, 128), F32) for _ in range(k + 1)), VEC)
        if halo:
            sweep(35, hi, outer, 0, halo)
        return accs

    def dot_index(i, k):
        return k * (k + 1) // 2 + i

    mid = square = None
    for step in range(2):
        viscous_pass(3 - step)
        if step == 0:
            for copy in halo_copies[8:]:
                copy.wait_recv()
            clear_second(TOP - HALO, keep_top)
            clear_second(BOT, keep_bot)
        accs = vector_pass(residual_at, 0, 3 - step)
        put_sum(0, accs[0])
        if step == 0:
            mid, square = basis_of(reduce_end(0), 0)
        rho = [None, 2.0 * square] + [square] * 3
        mid8, rho8 = mid, rho
        norm0 = accs[0]
        for k in range(KRYLOV):
            tangent_pass(k, ((3, 3, 2, 2, 1), (2, 1, 1, 1, 1))[step][k])
            accs = vector_pass(
                lambda r, n, k=k: jacobian_at(k, r, n, mid8, rho8[k]), k + 1, ((3, 2, 2, 2, 0), (1, 1, 1, 1, 0))[step][k]
            )
            for i, acc in enumerate(accs):
                put_sum(dot_index(i, k + 1), acc)
            if step == 0 and k == 0:
                def whole(acc):
                    return jnp.sum(jnp.sum(acc, axis=0, keepdims=True), axis=1, keepdims=True)

                g00, g01, g11 = whole(norm0), whole(accs[0]), whole(accs[1])
                m1 = mid[:, 0:1]
                alpha = (g01 + m1 * g00) / (g11 + 2.0 * m1 * g01 + m1 * m1 * g00 + 1e-12)
                alpha = jnp.broadcast_to(alpha, (8, 128))
                for i, acc in enumerate(estimate_pass(alpha)):
                    put_sum(N_DOTS + i, acc)

        reduce_a_start(1 + step, packed_sums(N_SUMS))
        reduce_b_start(1 + step)
        row = reduce_end(1 + step)
        gram = [[None] * 6 for _ in range(6)]
        for j in range(6):
            for i in range(j + 1):
                gram[i][j] = gram[j][i] = splat(row, dot_index(i, j))
        weights = small_solve(gram, mid, rho)

        def update(r, n, carry, step=step, weights=weights):
            tiles = pl.ds(0, 3 if step == 0 else 2)
            for c in range(2):
                total = fields[c, tiles, pl.ds(r, n), :]
                for k in range(KRYLOV):
                    total = total + weights[k] * krylov[k, c, tiles, pl.ds(r, n), :]
                fields[c, tiles, pl.ds(r, n), :] = total
            return carry

        if step == 0:
            for copy in halo_copies:
                copy.wait_send()
        lo, hi = strips(2 if step == 0 else 0)
        sweep(lo, hi, update, 0, UPD)
        if step == 0:
            mid, square = basis_of(row, N_DOTS)

    outs = []
    for t in range(2):
        outs.append(
            pltpu.make_async_copy(
                fields.at[pl.ds(0, 2), t, own_rows, :], out_ref.at[:, :, pl.ds(128 * t, 128)], out_sem.at[t]
            )
        )
        outs[-1].start()

    picks = []
    for s in range(8):
        picks.append([])
        for i in range(2):
            for j in range(2):
                hit = (ice_ref[i, j] > 0) & (owner_ref[i, j] * 2 + slot_ref[i, j] == s)
                picks[-1].append(jnp.where(hit, 1.0, 0.0).astype(F32))

    def choose(s, carry):
        src = pl.ds(pl.multiple_of(16 * s, 16), 16)
        for c in range(2):
            blocks = []
            for i in range(2):
                for j in range(2):
                    blocks.append(fields[c, j, pl.ds(pl.multiple_of(TOP + 128 * i + 16 * s, 16), 16), :])
            for slot in range(8):
                total = blocks[0] * picks[slot][0]
                for b in range(1, 4):
                    total = total + blocks[b] * picks[slot][b]
                send_blocks[slot // 2, slot % 2, c, src, :] = total
        return carry

    lax.fori_loop(0, 8, choose, 0)

    opposite = lax.rem(lat + 2, LAT)

    def held_copy(i, src, peer):
        copy = pltpu.make_async_remote_copy(
            src_ref=src, dst_ref=recv_blocks.at[i], send_sem=held_send.at[i], recv_sem=held_recv.at[i],
            device_id=(peer, lon), device_id_type=MESH,
        )
        copy.start()
        return copy

    held_copies = [
        held_copy(0, send_blocks.at[opposite, 0], south),
        held_copy(1, send_blocks.at[opposite, 1], north),
        held_copy(2, send_blocks.at[south, 1], south),
        held_copy(3, send_blocks.at[north, 0], north),
    ]

    def merge(i, owner, slot):
        def body(s, carry):
            r = pl.ds(pl.multiple_of(32 * s, 32), 32)
            for c in range(2):
                sum_blocks[i, c, r, :] = recv_blocks[i, c, r, :] + send_blocks[owner, slot, c, r, :]
            return carry

        lax.fori_loop(0, 4, body, 0)

    held_copies[0].wait_recv()
    merge(0, south, 0)
    held_copies.append(held_copy(4, sum_blocks.at[0], south))
    held_copies[1].wait_recv()
    merge(1, north, 1)
    held_copies.append(held_copy(5, sum_blocks.at[1], north))
    for copy in held_copies[2:]:
        copy.wait_recv()

    def collect(s, carry):
        r = pl.ds(pl.multiple_of(32 * s, 32), 32)
        for c in range(2):
            held_buf[0, c, r, :] = send_blocks[lat, 0, c, r, :] + (recv_blocks[3, c, r, :] + recv_blocks[4, c, r, :])
            held_buf[1, c, r, :] = send_blocks[lat, 1, c, r, :] + (recv_blocks[2, c, r, :] + recv_blocks[5, c, r, :])
        return carry

    lax.fori_loop(0, 4, collect, 0)
    last = pltpu.make_async_copy(held_buf, held_ref.at[:, 0], out_sem.at[2])
    last.start()

    for copy in held_copies:
        copy.wait_send()
    for inst in range(3):
        sent = buf_a.at[inst, 0]
        pltpu.make_async_copy(sent, sent, ar_send.at[inst, 0]).wait()
        sent = buf_b.at[inst, pl.ds(0, 63)]
        pltpu.make_async_copy(sent, sent, ar_send.at[inst, 1]).wait()
    for copy in outs:
        copy.wait()
    last.wait()


def on_device(velocity_old, wind_stress, strength, ice_mass, ice_mask, block_owner, block_slot):
    smem = pl.BlockSpec(memory_space=pltpu.SMEM)
    hbm = pl.BlockSpec(memory_space=pl.ANY)
    field = (3, ROWS, 128)
    velocity, held = pl.pallas_call(
        kernel,
        out_shape=(
            jax.ShapeDtypeStruct((2, 256, 256), F32),
            jax.ShapeDtypeStruct((2, 1, 2, 128, 128), F32),
        ),
        in_specs=[smem] * 3 + [hbm] * 4,
        out_specs=(hbm, hbm),
        scratch_shapes=[
            pltpu.VMEM((2, 2, 256, 128), F32),
            pltpu.VMEM((2, 2, 256, 128), F32),
            pltpu.VMEM((2, 256, 128), F32),
            pltpu.VMEM((2, 256, 128), F32),
            pltpu.VMEM((6,) + field, F32),
            pltpu.VMEM((3,) + field, F32),
            pltpu.VMEM((5,) + field, F32),
            pltpu.VMEM((3,) + field, F32),
            pltpu.VMEM((KRYLOV, 2) + field, F32),
            pltpu.VMEM((256, 128), F32),
            pltpu.VMEM((256, 128), F32),
            pltpu.VMEM((ROWS, 128), F32),
            pltpu.VMEM((ROWS, 128), F32),
            pltpu.VMEM((N_SUMS, 128), F32),
            pltpu.VMEM((3, 2, 1, 128), F32),
            pltpu.VMEM((3, 64, 1, 128), F32),
            pltpu.VMEM((4, 2, 2, 128, 128), F32),
            pltpu.VMEM((6, 2, 128, 128), F32),
            pltpu.VMEM((2, 2, 128, 128), F32),
            pltpu.VMEM((2, 2, 128, 128), F32),
            pltpu.SemaphoreType.DMA((8,)),
            pltpu.SemaphoreType.DMA((10,)),
            pltpu.SemaphoreType.DMA((10,)),
            pltpu.SemaphoreType.DMA((3, 2)),
            pltpu.SemaphoreType.DMA((3, 2)),
            pltpu.SemaphoreType.DMA((6,)),
            pltpu.SemaphoreType.DMA((6,)),
            pltpu.SemaphoreType.DMA((3,)),
        ],
        compiler_params=pltpu.CompilerParams(
            collective_id=0, has_side_effects=True, vmem_limit_bytes=56 * 1024 * 1024
        ),
    )(ice_mask, block_owner, block_slot, velocity_old, wind_stress, strength, ice_mass)
    return velocity, held


def solution(mesh):
    return jax.shard_map(
        on_device,
        mesh=mesh,
        in_specs=(
            P(None, "lat", "lon"),
            P(None, "lat", "lon"),
            P("lat", "lon"),
            P("lat", "lon"),
            P("lat", "lon"),
            P("lat", "lon"),
            P("lat", "lon"),
        ),
        out_specs=(P(None, "lat", "lon"), P("lat", "lon", None, None, None)),
        check_vma=False,
    )
```

```python
import functools

import jax
import jax.numpy as jnp
from jax import lax
from jax.experimental import pallas as pl
from jax.experimental.pallas import tpu as pltpu
from jax.sharding import PartitionSpec as P

MESH = pl.DeviceIdType.MESH
F32 = jnp.float32

KRYLOV = 5
TINY_SQ = 1e-6
LAT = 4
LON = 32

ROWS = 320
TOP = 32
BOT = 288
HALO = 24
OWN_STRIPS = 32

WIDTHS = (22, 22, 22, 20, 20, 20)
OFFSETS = (0, 22, 44, 66, 86, 106)

VISC = 10
TAN = 19
VEC = 32
UPD = 4

N_DOTS = 21
N_SUMS = 24


def lanes(shape):
    return lax.broadcasted_iota(jnp.int32, shape, len(shape) - 1)


def sweep(lo, hi, body, carry, strips):
    count, rest = divmod(hi - lo, strips)

    def step(i, carry):
        return body(pl.multiple_of(8 + 8 * lo + 8 * strips * i, 8), 8 * strips, carry)

    if count:
        carry = lax.fori_loop(0, count, step, carry)
    if rest:
        carry = body(8 + 8 * (hi - rest), 8 * rest, carry)
    return carry


def fold(x):
    x = x.reshape(-1, 8, 128)
    total = x[0]
    for i in range(1, x.shape[0]):
        total = total + x[i]
    return total


def rows8(start):
    return pl.ds(start, 8)


def diff_x(f):
    lane = lanes((1,) + f.shape[1:])
    right = pltpu.roll(f, 127, 2)
    left = pltpu.roll(f, 1, 2)
    right_next = jnp.concatenate([right[1:], right[:1]], axis=0)
    left_next = jnp.concatenate([left[2:], left[:2]], axis=0)
    return jnp.where(lane == 127, right_next, right) - jnp.where(lane == 0, left_next, left)


def diff_x_rough(f):
    return pltpu.roll(f, 127, 2) - pltpu.roll(f, 1, 2)


def coefficients(sum_rate, differ, shear, pressure):
    q = 0.25 * (sum_rate * sum_rate) + 0.0625 * (differ * differ + shear * shear)
    inv = lax.rsqrt(q + 0.04)
    bulk = 0.5 * pressure * inv
    weight = inv * jnp.sqrt(0.5 * bulk)
    eighth = 0.125 * weight
    return 0.5 * bulk, 0.125 * bulk, (0.5 * weight) * sum_rate, eighth * differ, eighth * shear


def spectrum_sums(m2, gs, gf, ge, mass, turn):
    diag = mass + 1.5 * m2 - (gs * gs + gf * gf + ge * ge)
    c11 = 2.5 * m2 - 2.0 * (gs + gf) * (gs + gf)
    c22 = 2.5 * m2 - 2.0 * (gs - gf) * (gs - gf)
    c33 = 2.0 * m2 - 8.0 * ge * ge
    spread = diag * diag + turn * turn + 0.0625 * (c11 * c11 + c22 * c22) + 0.03125 * (c33 * c33)
    return diag, spread


def splat(row, index):
    return jnp.broadcast_to(row[:, index : index + 1], (1, 128))


def wide(row):
    return jnp.broadcast_to(row, (8, 128))


def small_solve(gram, mid, rho):
    def dot(u, gv):
        total = None
        for x, y in zip(u, gv):
            if x is not None:
                total = x * y if total is None else total + x * y
        return total

    def times_gram(u, count):
        return [dot(u, [gram[i][j] for j in range(6)]) for i in range(count)]

    def apply(c):
        out = [None] * 6
        for k, x in enumerate(c):
            if x is None:
                continue
            if k < 5:
                terms = [(k + 1, x), (k, mid * x)]
                if k > 0:
                    terms.append((k - 1, rho[k] * x))
                for at, term in terms:
                    out[at] = term if out[at] is None else out[at] + term
        return out

    beta = jnp.sqrt(gram[0][0] + TINY_SQ)
    basis = [[1.0 / beta] + [None] * 5]
    upper = []
    cosines, sines = [], []
    target = [beta]
    for j in range(KRYLOV):
        u = apply(basis[j])
        gu = times_gram(u, j + 2)
        coeffs = [dot(basis[i][: j + 2], gu) for i in range(j + 1)]
        for i in range(j + 1):
            u = [
                x if y is None else x - coeffs[i] * y
                for x, y in zip(u, basis[i])
            ]
        gu = times_gram(u, j + 2)
        square = jnp.maximum(dot(u[: j + 2], gu), 0.0)
        length = jnp.sqrt(square + TINY_SQ)
        inv_length = 1.0 / length
        basis.append([None if x is None else x * inv_length for x in u])
        column = coeffs + [length]
        for i in range(j):
            a, b = column[i], column[i + 1]
            column[i] = cosines[i] * a + sines[i] * b
            column[i + 1] = cosines[i] * b - sines[i] * a
        a, b = column[j], column[j + 1]
        inv_radius = 1.0 / jnp.sqrt(a * a + b * b)
        cosine, sine = a * inv_radius, b * inv_radius
        cosines.append(cosine)
        sines.append(sine)
        column[j] = cosine * a + sine * b
        upper.append(column[: j + 1])
        target.append(-sine * target[j])
        target[j] = cosine * target[j]
    weights = [None] * KRYLOV
    for j in reversed(range(KRYLOV)):
        known = target[j]
        for k in range(j + 1, KRYLOV):
            known = known - upper[k][j] * weights[k]
        weights[j] = known / upper[j][j]
    out = []
    for k in range(KRYLOV):
        total = None
        for j in range(k, KRYLOV):
            term = weights[j] * basis[j][k]
            total = term if total is None else total + term
        out.append(total)
    return out


def kernel(
    ice_ref, owner_ref, slot_ref, vel_ref, wind_ref, strength_ref, mass_ref,
    out_ref, held_ref,
    st_vel, st_wind, st_strength, st_mass,
    fields, local, coef, stress, krylov,
    pack_e, pack_w, got_l, got_r, sums,
    buf_a, buf_b, send_blocks, recv_blocks, sum_blocks,
    in_sem, halo_send, halo_recv, ar_send, ar_recv, held_send, held_recv,
):
    lat, lon = lax.axis_index("lat"), lax.axis_index("lon")
    north, south = lax.rem(lat + LAT - 1, LAT), lax.rem(lat + 1, LAT)
    east, west = lax.rem(lon + 1, LON), lax.rem(lon + LON - 1, LON)
    core = lax.rem(lon, 2)
    chip = lon // 2
    rank_b = lat * 16 + chip
    y, z = chip // 4, lax.rem(chip, 4)

    partner = (lat, chip * 2 + (1 - core))
    peers_b = []
    shifts = [(i, j, k) for i in range(4) for j in range(4) for k in range(4) if i or j or k]
    for i, j, k in sorted(shifts, key=lambda d: -sum(min(n, 4 - n) + (n > 0) for n in d)):
        other = lax.rem(y + j, 4) * 4 + lax.rem(z + k, 4)
        peers_b.append((lax.rem(lat + i, 4), other * 2 + core))
    halo_peers = [(lat, east), (lat, west), (north, east), (north, west), (south, east), (south, west)]

    loads = []
    for t in range(2):
        cols = pl.ds(128 * t, 128)
        loads.append(pltpu.make_async_copy(vel_ref.at[:, :, cols], st_vel.at[:, t], in_sem.at[t]))
        loads.append(pltpu.make_async_copy(wind_ref.at[:, :, cols], st_wind.at[:, t], in_sem.at[2 + t]))
        loads.append(pltpu.make_async_copy(strength_ref.at[:, cols], st_strength.at[t], in_sem.at[4 + t]))
        loads.append(pltpu.make_async_copy(mass_ref.at[:, cols], st_mass.at[t], in_sem.at[6 + t]))
    for copy in loads:
        copy.start()

    barrier = pltpu.get_barrier_semaphore()
    greeted = peers_b + halo_peers
    for peer in greeted:
        pl.semaphore_signal(barrier, inc=1, device_id=peer, device_id_type=MESH)

    for copy in loads:
        copy.wait()

    ice = [[ice_ref[i, j].astype(F32) for j in range(2)] for i in range(2)]
    for half in range(2):

        def prepare(s, carry, half=half):
            src = pl.ds(pl.multiple_of(32 * s, 32), 32)
            dst = pl.ds(pl.multiple_of(TOP + 32 * s, 32), 32)
            lane = lanes((32, 128))
            for t in range(2):
                w = ice[half][t]
                mass = st_mass[t, src, :] * w
                v_e = st_vel[0, t, src, :]
                v_n = st_vel[1, t, src, :]
                values = (
                    v_e * w,
                    v_n * w,
                    st_strength[t, src, :] * w,
                    mass,
                    mass * v_e + w * st_wind[0, t, src, :],
                    mass * v_n + w * st_wind[1, t, src, :],
                )
                for f in range(6):
                    fields[f, t, dst, :] = values[f]
                local[0, t, dst, :] = mass + 0.5 * w
                local[1, t, dst, :] = 0.3 * mass
                local[2, t, dst, :] = jnp.zeros((32, 128), F32) + 0.5 * w
                packed = None
                for f in range(6):
                    turn = (OFFSETS[f] if t == 0 else OFFSETS[f] + WIDTHS[f]) % 128
                    rolled = values[f] if turn == 0 else pltpu.roll(values[f], turn, 1)
                    packed = rolled if f == 0 else jnp.where(lane >= OFFSETS[f], rolled, packed)
                (pack_w if t == 0 else pack_e)[src, :] = packed
            return carry

        lax.fori_loop(4 * half, 4 * half + 4, prepare, 0)

    first, second, both = pl.ds(0, 3), pl.ds(3, 3), pl.ds(0, 2)
    def reduce_a_start(inst, row):
        buf_a[inst, core] = row
        pltpu.make_async_remote_copy(
            src_ref=buf_a.at[inst, core], dst_ref=buf_a.at[inst, core],
            send_sem=ar_send.at[inst, 0], recv_sem=ar_recv.at[inst, 0],
            device_id=partner, device_id_type=MESH,
        ).start()

    def reduce_b_start(inst):
        waited = buf_a.at[inst, 0]
        pltpu.make_async_copy(waited, waited, ar_recv.at[inst, 0]).wait()
        buf_b[inst, rank_b] = buf_a[inst, 0] + buf_a[inst, 1]
        for peer in peers_b:
            pltpu.make_async_remote_copy(
                src_ref=buf_b.at[inst, rank_b], dst_ref=buf_b.at[inst, rank_b],
                send_sem=ar_send.at[inst, 1], recv_sem=ar_recv.at[inst, 1],
                device_id=peer, device_id_type=MESH,
            ).start()

    def reduce_end(inst):
        waited = buf_b.at[inst, pl.ds(0, 63)]
        pltpu.make_async_copy(waited, waited, ar_recv.at[inst, 1]).wait()
        parts = [buf_b[inst, pl.ds(8 * i, 8)] for i in range(8)]
        while len(parts) > 1:
            parts = [x + y for x, y in zip(parts[::2], parts[1::2])]
        return jnp.sum(parts[0], axis=0)

    def put_sum(index, acc):
        sums[index : index + 1, :] = jnp.sum(acc, axis=0, keepdims=True)

    def packed_sums(count):
        m = sums[0:count, :]
        total = jnp.sum(m, axis=1, keepdims=True)
        sub = lax.broadcasted_iota(jnp.int32, (count, 128), 0)
        spread = jnp.where(lanes((count, 128)) == sub, total, 0.0)
        return jnp.sum(spread, axis=0, keepdims=True)

    def estimate_pass(alpha, count):
        def at(c, r):
            flow = fields[c, both, rows8(r), :]
            return flow if alpha is None else flow + alpha * krylov[0, c, both, rows8(r), :]

        def one(r, carry):
            diag_acc, spread_acc, ice_acc = carry
            x_e, x_n = diff_x_rough(at(0, r)), diff_x_rough(at(1, r))
            y_e, y_n = at(0, r + 1) - at(0, r - 1), at(1, r + 1) - at(1, r - 1)
            m2, _, gs, gf, ge = coefficients(x_e + y_n, x_e - y_n, y_e + x_n, fields[2, both, rows8(r), :])
            diag, spread = spectrum_sums(
                m2, gs, gf, ge, local[0, both, rows8(r), :], local[1, both, rows8(r), :]
            )
            weight = local[2, both, rows8(r), :]
            return (
                diag_acc + (diag[0] + diag[1]),
                spread_acc + (spread[0] + spread[1]),
                ice_acc + 2.0 * (weight[0] + weight[1]),
            )

        def body(i, carry):
            for j in range(5):
                carry = one(pl.multiple_of(TOP + 8 + 48 * j + 16 * i, 8), carry)
            return carry

        zero = jnp.zeros((8, 128), F32)
        return lax.fori_loop(0, count, body, (zero, zero, zero))

    def basis_of(row, at):
        diag, spread, count = splat(row, at), splat(row, at + 1), splat(row, at + 2)
        inv = 1.0 / jnp.maximum(count, 1.0)
        mid = diag * inv
        return mid, jnp.maximum(spread * inv - mid * mid, 0.01)

    for i, acc in enumerate(estimate_pass(None, 3)):
        put_sum(i, acc)
    first_sums = packed_sums(8)

    pl.semaphore_wait(barrier, len(greeted))

    own_top, own_bot = pl.ds(TOP, HALO), pl.ds(BOT - HALO, HALO)
    halo_top, halo_bot = pl.ds(TOP - HALO, HALO), pl.ds(BOT, HALO)
    own_rows = pl.ds(TOP, 256)
    src_top, src_bot = pl.ds(0, HALO), pl.ds(256 - HALO, HALO)
    plan = [
        (fields.at[first, both, own_top, :], fields.at[first, both, halo_bot, :], (north, lon)),
        (fields.at[first, both, own_bot, :], fields.at[first, both, halo_top, :], (south, lon)),
        (pack_e.at[src_top, :], got_l.at[halo_bot, :], (north, east)),
        (pack_w.at[src_top, :], got_r.at[halo_bot, :], (north, west)),
        (pack_e.at[src_bot, :], got_l.at[halo_top, :], (south, east)),
        (pack_w.at[src_bot, :], got_r.at[halo_top, :], (south, west)),
        (pack_e, got_l.at[own_rows, :], (lat, east)),
        (pack_w, got_r.at[own_rows, :], (lat, west)),
        (fields.at[second, both, own_top, :], fields.at[second, both, halo_bot, :], (north, lon)),
        (fields.at[second, both, own_bot, :], fields.at[second, both, halo_top, :], (south, lon)),
    ]
    halo_copies = []
    for i, (src, dst, peer) in enumerate(plan):
        copy = pltpu.make_async_remote_copy(
            src_ref=src, dst_ref=dst, send_sem=halo_send.at[i], recv_sem=halo_recv.at[i],
            device_id=peer, device_id_type=MESH,
        )
        copy.start()
        halo_copies.append(copy)

    reduce_a_start(0, first_sums)

    keep_top = jnp.where(lat == 0, 0.0, 1.0).astype(F32)
    keep_bot = jnp.where(lat == LAT - 1, 0.0, 1.0).astype(F32)

    def put_local(t, here, mass):
        w = jnp.where(mass > 0.0, 1.0, 0.0)
        local[0, t, here, :] = mass + 0.5 * w
        local[1, t, here, :] = 0.3 * mass
        local[2, t, here, :] = 0.5 * w

    def unpack(keep):
        def body(r, n, carry):
            here = pl.ds(r, n)
            left, right = got_l[here, :], got_r[here, :]
            lane = lanes((n, 128))
            for f in range(6):
                turn_l = (128 - OFFSETS[f] - WIDTHS[f]) % 128
                turn_r = (128 - OFFSETS[f]) % 128
                from_l = left if turn_l == 0 else pltpu.roll(left, turn_l, 1)
                from_r = right if turn_r == 0 else pltpu.roll(right, turn_r, 1)
                merged = jnp.where(lane < 64, from_r, from_l)
                if keep is not None:
                    merged = merged * keep
                fields[f, 2, here, :] = merged
                if f == 3:
                    put_local(2, here, merged)
            return carry

        return body

    def clear_first(top, keep):
        fields[first, both, pl.ds(top, HALO), :] = fields[first, both, pl.ds(top, HALO), :] * keep

    def clear_second(top, keep):
        here = pl.ds(top, HALO)
        for t in range(2):
            for f in range(3, 6):
                kept = fields[f, t, here, :] * keep
                fields[f, t, here, :] = kept
                if f == 3:
                    put_local(t, here, kept)

    for copy in halo_copies[:8]:
        copy.wait_recv()
    sweep(0, 3, unpack(keep_top), 0, 3)
    sweep(3, 35, unpack(None), 0, 4)
    sweep(35, 38, unpack(keep_bot), 0, 3)
    clear_first(TOP - HALO, keep_top)
    clear_first(BOT, keep_bot)

    reduce_b_start(0)

    def strips(halo):
        return 3 - halo, 35 + halo

    def viscous_pass(halo):
        def body(r, n, carry):
            here, up, down = pl.ds(r, n), pl.ds(r + 1, n), pl.ds(r - 1, n)
            x_e, x_n = diff_x(fields[0, :, here, :]), diff_x(fields[1, :, here, :])
            y_e = fields[0, :, up, :] - fields[0, :, down, :]
            y_n = fields[1, :, up, :] - fields[1, :, down, :]
            pressure = fields[2, :, here, :]
            total, differ, shear = x_e + y_n, x_e - y_n, y_e + x_n
            values = coefficients(total, differ, shear, pressure)
            for i in range(5):
                coef[i, :, here, :] = values[i]
            p, n = values[0] * total - 0.5 * pressure, values[1] * differ
            stress[0, :, here, :] = p + n
            stress[1, :, here, :] = p - n
            stress[2, :, here, :] = values[1] * shear
            return carry

        lo, hi = strips(halo)
        sweep(lo, hi, body, 0, VISC)

    def tangent_pass(k, halo):
        def body(r, n, carry):
            here, up, down = pl.ds(r, n), pl.ds(r + 1, n), pl.ds(r - 1, n)
            x_e, x_n = diff_x(krylov[k, 0, :, here, :]), diff_x(krylov[k, 1, :, here, :])
            y_e = krylov[k, 0, :, up, :] - krylov[k, 0, :, down, :]
            y_n = krylov[k, 1, :, up, :] - krylov[k, 1, :, down, :]
            total, differ, shear = x_e + y_n, x_e - y_n, y_e + x_n
            gs, gf, ge = coef[2, :, here, :], coef[3, :, here, :], coef[4, :, here, :]
            q = gs * total + gf * differ + ge * shear
            m8 = coef[1, :, here, :]
            p = coef[0, :, here, :] * total - q * gs
            n = m8 * differ - q * gf
            stress[0, :, here, :] = p + n
            stress[1, :, here, :] = p - n
            stress[2, :, here, :] = m8 * shear - q * ge
            return carry

        lo, hi = strips(halo)
        sweep(lo, hi, body, 0, TAN)

    def stress_force(r, n):
        here, up, down = pl.ds(r, n), pl.ds(r + 1, n), pl.ds(r - 1, n)
        t11, t12 = stress[0, :, here, :], stress[2, :, here, :]
        y12 = stress[2, :, up, :] - stress[2, :, down, :]
        y22 = stress[1, :, up, :] - stress[1, :, down, :]
        half = local[2, :, here, :]
        return half * (diff_x(t11) + y12), half * (diff_x(t12) + y22)

    def residual_at(r, n):
        here = pl.ds(r, n)
        force_e, force_n = stress_force(r, n)
        mass, turn = local[0, :, here, :], local[1, :, here, :]
        a, b = fields[0, :, here, :], fields[1, :, here, :]
        r_e = fields[4, :, here, :] + force_e - (mass * a - turn * b)
        r_n = fields[5, :, here, :] + force_n - (mass * b + turn * a)
        return r_e, r_n

    def jacobian_at(k, r, n, mid, rho):
        here = pl.ds(r, n)
        force_e, force_n = stress_force(r, n)
        mass, turn = local[0, :, here, :] - mid, local[1, :, here, :]
        c, d = krylov[k, 0, :, here, :], krylov[k, 1, :, here, :]
        w_e = (mass * c - turn * d) - force_e
        w_n = (mass * d + turn * c) - force_n
        if k > 0:
            w_e = w_e - rho * krylov[k - 1, 0, :, here, :]
            w_n = w_n - rho * krylov[k - 1, 1, :, here, :]
        return w_e, w_n

    def vector_pass(make, k, halo):
        stored = k < KRYLOV

        def put(r, n):
            v_e, v_n = make(r, n)
            if stored:
                krylov[k, 0, :, pl.ds(r, n), :] = v_e
                krylov[k, 1, :, pl.ds(r, n), :] = v_n
            return v_e, v_n

        def outer(r, n, carry):
            put(r, n)
            return carry

        def inner(r, n, accs):
            v_e, v_n = put(r, n)
            v_e, v_n = v_e[:2], v_n[:2]
            out = []
            for i in range(k + 1):
                if i < k:
                    u_e = krylov[i, 0, pl.ds(0, 2), pl.ds(r, n), :]
                    u_n = krylov[i, 1, pl.ds(0, 2), pl.ds(r, n), :]
                else:
                    u_e, u_n = v_e, v_n
                out.append(accs[i] + fold(u_e * v_e + u_n * v_n))
            return tuple(out)

        lo, hi = strips(halo)
        if halo:
            sweep(lo, 3, outer, 0, halo)
        accs = sweep(3, 35, inner, tuple(jnp.zeros((8, 128), F32) for _ in range(k + 1)), VEC)
        if halo:
            sweep(35, hi, outer, 0, halo)
        return accs

    def dot_index(i, k):
        return k * (k + 1) // 2 + i

    mid = square = None
    for step in range(2):
        viscous_pass(3 - step)
        if step == 0:
            for copy in halo_copies[8:]:
                copy.wait_recv()
            clear_second(TOP - HALO, keep_top)
            clear_second(BOT, keep_bot)
        accs = vector_pass(residual_at, 0, 3 - step)
        put_sum(0, accs[0])
        if step == 0:
            mid, square = basis_of(reduce_end(0), 0)
        rho = [None, 2.0 * square] + [square] * 3
        mid8, rho8 = mid, rho
        norm0 = accs[0]
        for k in range(KRYLOV):
            tangent_pass(k, ((3, 3, 2, 2, 1), (2, 1, 1, 1, 1))[step][k])
            accs = vector_pass(
                lambda r, n, k=k: jacobian_at(k, r, n, mid8, rho8[k]), k + 1, ((3, 2, 2, 2, 0), (1, 1, 1, 1, 0))[step][k]
            )
            for i, acc in enumerate(accs):
                put_sum(dot_index(i, k + 1), acc)
            if step == 0 and k == 0:
                def whole(acc):
                    return jnp.sum(jnp.sum(acc, axis=0, keepdims=True), axis=1, keepdims=True)

                g00, g01, g11 = whole(norm0), whole(accs[0]), whole(accs[1])
                m1 = mid[:, 0:1]
                alpha = (g01 + m1 * g00) / (g11 + 2.0 * m1 * g01 + m1 * m1 * g00 + 1e-12)
                alpha = jnp.broadcast_to(alpha, (8, 128))
                for i, acc in enumerate(estimate_pass(alpha, 1)):
                    put_sum(N_DOTS + i, acc)

        reduce_a_start(1 + step, packed_sums(N_SUMS))
        reduce_b_start(1 + step)
        row = reduce_end(1 + step)
        gram = [[None] * 6 for _ in range(6)]
        for j in range(6):
            for i in range(j + 1):
                gram[i][j] = gram[j][i] = splat(row, dot_index(i, j))
        weights = small_solve(gram, mid, rho)

        def update(r, n, carry, step=step, weights=weights):
            tiles = pl.ds(0, 3 if step == 0 else 2)
            for c in range(2):
                total = fields[c, tiles, pl.ds(r, n), :]
                for k in range(KRYLOV):
                    total = total + weights[k] * krylov[k, c, tiles, pl.ds(r, n), :]
                if step == 0:
                    fields[c, tiles, pl.ds(r, n), :] = total
                else:
                    for t in range(2):
                        out_ref[c, pl.ds(r - TOP, n), pl.ds(128 * t, 128)] = total[t]
            return carry

        if step == 0:
            for copy in halo_copies:
                copy.wait_send()
        lo, hi = strips(2 if step == 0 else 0)
        sweep(lo, hi, update, 0, UPD)
        if step == 0:
            mid, square = basis_of(row, N_DOTS)

    picks = []
    for s in range(8):
        picks.append([])
        for i in range(2):
            for j in range(2):
                hit = (ice_ref[i, j] > 0) & (owner_ref[i, j] * 2 + slot_ref[i, j] == s)
                picks[-1].append(jnp.where(hit, 1.0, 0.0).astype(F32))

    def choose(s, carry):
        src = pl.ds(pl.multiple_of(16 * s, 16), 16)
        for c in range(2):
            blocks = []
            for i in range(2):
                for j in range(2):
                    blocks.append(out_ref[c, pl.ds(pl.multiple_of(128 * i + 16 * s, 16), 16), pl.ds(128 * j, 128)])
            for slot in range(8):
                total = blocks[0] * picks[slot][0]
                for b in range(1, 4):
                    total = total + blocks[b] * picks[slot][b]
                send_blocks[slot // 2, slot % 2, c, src, :] = total
        return carry

    lax.fori_loop(0, 8, choose, 0)

    opposite = lax.rem(lat + 2, LAT)

    def held_copy(i, src, peer):
        copy = pltpu.make_async_remote_copy(
            src_ref=src, dst_ref=recv_blocks.at[i], send_sem=held_send.at[i], recv_sem=held_recv.at[i],
            device_id=(peer, lon), device_id_type=MESH,
        )
        copy.start()
        return copy

    held_copies = [
        held_copy(0, send_blocks.at[opposite, 0], south),
        held_copy(1, send_blocks.at[opposite, 1], north),
        held_copy(2, send_blocks.at[south, 1], south),
        held_copy(3, send_blocks.at[north, 0], north),
    ]

    def merge(i, owner, slot):
        def body(s, carry):
            r = pl.ds(pl.multiple_of(32 * s, 32), 32)
            for c in range(2):
                sum_blocks[i, c, r, :] = recv_blocks[i, c, r, :] + send_blocks[owner, slot, c, r, :]
            return carry

        lax.fori_loop(0, 4, body, 0)

    held_copies[0].wait_recv()
    merge(0, south, 0)
    held_copies.append(held_copy(4, sum_blocks.at[0], south))
    held_copies[1].wait_recv()
    merge(1, north, 1)
    held_copies.append(held_copy(5, sum_blocks.at[1], north))
    for copy in held_copies[2:]:
        copy.wait_recv()

    def collect(s, carry):
        r = pl.ds(pl.multiple_of(32 * s, 32), 32)
        for c in range(2):
            held_ref[0, 0, c, r, :] = send_blocks[lat, 0, c, r, :] + (recv_blocks[3, c, r, :] + recv_blocks[4, c, r, :])
            held_ref[1, 0, c, r, :] = send_blocks[lat, 1, c, r, :] + (recv_blocks[2, c, r, :] + recv_blocks[5, c, r, :])
        return carry

    lax.fori_loop(0, 4, collect, 0)

    for copy in held_copies:
        copy.wait_send()
    for inst in range(3):
        sent = buf_a.at[inst, 0]
        pltpu.make_async_copy(sent, sent, ar_send.at[inst, 0]).wait()
        sent = buf_b.at[inst, pl.ds(0, 63)]
        pltpu.make_async_copy(sent, sent, ar_send.at[inst, 1]).wait()


def on_device(velocity_old, wind_stress, strength, ice_mass, ice_mask, block_owner, block_slot):
    smem = pl.BlockSpec(memory_space=pltpu.SMEM)
    hbm = pl.BlockSpec(memory_space=pl.ANY)
    vm = pl.BlockSpec(memory_space=pltpu.VMEM)
    field = (3, ROWS, 128)
    velocity, held = pl.pallas_call(
        kernel,
        out_shape=(pltpu.VMEM((2, 256, 256), F32), pltpu.VMEM((2, 1, 2, 128, 128), F32)),
        in_specs=[smem] * 3 + [pl.BlockSpec(memory_space=pltpu.HBM)] * 4,
        out_specs=(vm, vm),
        scratch_shapes=[
            pltpu.VMEM((2, 2, 256, 128), F32),
            pltpu.VMEM((2, 2, 256, 128), F32),
            pltpu.VMEM((2, 256, 128), F32),
            pltpu.VMEM((2, 256, 128), F32),
            pltpu.VMEM((6,) + field, F32),
            pltpu.VMEM((3,) + field, F32),
            pltpu.VMEM((5,) + field, F32),
            pltpu.VMEM((3,) + field, F32),
            pltpu.VMEM((KRYLOV, 2) + field, F32),
            pltpu.VMEM((256, 128), F32),
            pltpu.VMEM((256, 128), F32),
            pltpu.VMEM((ROWS, 128), F32),
            pltpu.VMEM((ROWS, 128), F32),
            pltpu.VMEM((N_SUMS, 128), F32),
            pltpu.VMEM((3, 2, 1, 128), F32),
            pltpu.VMEM((3, 64, 1, 128), F32),
            pltpu.VMEM((4, 2, 2, 128, 128), F32),
            pltpu.VMEM((6, 2, 128, 128), F32),
            pltpu.VMEM((2, 2, 128, 128), F32),
            pltpu.SemaphoreType.DMA((8,)),
            pltpu.SemaphoreType.DMA((10,)),
            pltpu.SemaphoreType.DMA((10,)),
            pltpu.SemaphoreType.DMA((3, 2)),
            pltpu.SemaphoreType.DMA((3, 2)),
            pltpu.SemaphoreType.DMA((6,)),
            pltpu.SemaphoreType.DMA((6,)),
        ],
        compiler_params=pltpu.CompilerParams(
            collective_id=0, has_side_effects=True, vmem_limit_bytes=56 * 1024 * 1024
        ),
    )(ice_mask, block_owner, block_slot, velocity_old, wind_stress, strength, ice_mass)

    def pass_on(velocity_ref, held_ref, velocity_out, held_out, sem):
        copies = [
            pltpu.make_async_copy(velocity_ref, velocity_out, sem.at[0]),
            pltpu.make_async_copy(held_ref, held_out, sem.at[1]),
        ]
        for copy in copies:
            copy.start()
        for copy in copies:
            copy.wait()

    return pl.pallas_call(
        pass_on,
        out_shape=(
            jax.ShapeDtypeStruct((2, 256, 256), F32),
            jax.ShapeDtypeStruct((2, 1, 2, 128, 128), F32),
        ),
        in_specs=[hbm] * 2,
        out_specs=(hbm, hbm),
        scratch_shapes=[pltpu.SemaphoreType.DMA((2,))],
        compiler_params=pltpu.CompilerParams(vmem_limit_bytes=4 * 1024 * 1024),
    )(velocity, held)


def solution(mesh):
    return jax.shard_map(
        on_device,
        mesh=mesh,
        in_specs=(
            P(None, "lat", "lon"),
            P(None, "lat", "lon"),
            P("lat", "lon"),
            P("lat", "lon"),
            P("lat", "lon"),
            P("lat", "lon"),
            P("lat", "lon"),
        ),
        out_specs=(P(None, "lat", "lon"), P("lat", "lon", None, None, None)),
        check_vma=False,
    )
```

```python
import functools

import jax
import jax.numpy as jnp
from jax import lax
from jax.experimental import pallas as pl
from jax.experimental.pallas import tpu as pltpu
from jax.sharding import PartitionSpec as P

MESH = pl.DeviceIdType.MESH
F32 = jnp.float32

KRYLOV = 5
TINY_SQ = 1e-6
LAT = 4
LON = 32

ROWS = 320
TOP = 32
BOT = 288
HALO = 24
OWN_STRIPS = 32

WIDTHS = (22, 22, 22, 20, 20, 20)
OFFSETS = (0, 22, 44, 66, 86, 106)

VISC = 10
TAN = 10
VEC = 16
UPD = 4
SUB = 2

N_DOTS = 21
N_SUMS = 24


def lanes(shape):
    return lax.broadcasted_iota(jnp.int32, shape, len(shape) - 1)


def sweep(lo, hi, body, carry, strips):
    count, rest = divmod(hi - lo, strips)

    def step(i, carry):
        first = pl.multiple_of(8 + 8 * lo + 8 * strips * i, 8)
        for j in range(0, strips, SUB):
            carry = body(first + 8 * j, 8 * min(SUB, strips - j), carry)
        return carry

    if count:
        carry = lax.fori_loop(0, count, step, carry)
    if rest:
        carry = body(8 + 8 * (hi - rest), 8 * rest, carry)
    return carry


def fold(x):
    x = x.reshape(-1, 8, 128)
    total = x[0]
    for i in range(1, x.shape[0]):
        total = total + x[i]
    return total


def rows8(start):
    return pl.ds(start, 8)


def diff_x(f):
    lane = lanes((1,) + f.shape[1:])
    right = pltpu.roll(f, 127, 2)
    left = pltpu.roll(f, 1, 2)
    right_next = jnp.concatenate([right[1:], right[:1]], axis=0)
    left_next = jnp.concatenate([left[2:], left[:2]], axis=0)
    return jnp.where(lane == 127, right_next, right) - jnp.where(lane == 0, left_next, left)


def diff_x_rough(f):
    return pltpu.roll(f, 127, 2) - pltpu.roll(f, 1, 2)


def coefficients(sum_rate, differ, shear, pressure):
    q = 0.25 * (sum_rate * sum_rate) + 0.0625 * (differ * differ + shear * shear)
    inv = lax.rsqrt(q + 0.04)
    bulk = 0.5 * pressure * inv
    weight = inv * jnp.sqrt(0.5 * bulk)
    eighth = 0.125 * weight
    return 0.5 * bulk, 0.125 * bulk, (0.5 * weight) * sum_rate, eighth * differ, eighth * shear


def spectrum_sums(m2, gs, gf, ge, mass, turn):
    diag = mass + 1.5 * m2 - (gs * gs + gf * gf + ge * ge)
    c11 = 2.5 * m2 - 2.0 * (gs + gf) * (gs + gf)
    c22 = 2.5 * m2 - 2.0 * (gs - gf) * (gs - gf)
    c33 = 2.0 * m2 - 8.0 * ge * ge
    spread = diag * diag + turn * turn + 0.0625 * (c11 * c11 + c22 * c22) + 0.03125 * (c33 * c33)
    return diag, spread


def splat(row, index):
    return jnp.broadcast_to(row[:, index : index + 1], (1, 128))


def wide(row):
    return jnp.broadcast_to(row, (8, 128))


def small_solve(gram, mid, rho):
    def dot(u, gv):
        total = None
        for x, y in zip(u, gv):
            if x is not None:
                total = x * y if total is None else total + x * y
        return total

    def times_gram(u, count):
        return [dot(u, [gram[i][j] for j in range(6)]) for i in range(count)]

    def apply(c):
        out = [None] * 6
        for k, x in enumerate(c):
            if x is None:
                continue
            if k < 5:
                terms = [(k + 1, x), (k, mid * x)]
                if k > 0:
                    terms.append((k - 1, rho[k] * x))
                for at, term in terms:
                    out[at] = term if out[at] is None else out[at] + term
        return out

    beta = jnp.sqrt(gram[0][0] + TINY_SQ)
    basis = [[1.0 / beta] + [None] * 5]
    upper = []
    cosines, sines = [], []
    target = [beta]
    for j in range(KRYLOV):
        u = apply(basis[j])
        gu = times_gram(u, j + 2)
        coeffs = [dot(basis[i][: j + 2], gu) for i in range(j + 1)]
        for i in range(j + 1):
            u = [
                x if y is None else x - coeffs[i] * y
                for x, y in zip(u, basis[i])
            ]
        gu = times_gram(u, j + 2)
        square = jnp.maximum(dot(u[: j + 2], gu), 0.0)
        length = jnp.sqrt(square + TINY_SQ)
        inv_length = 1.0 / length
        basis.append([None if x is None else x * inv_length for x in u])
        column = coeffs + [length]
        for i in range(j):
            a, b = column[i], column[i + 1]
            column[i] = cosines[i] * a + sines[i] * b
            column[i + 1] = cosines[i] * b - sines[i] * a
        a, b = column[j], column[j + 1]
        inv_radius = 1.0 / jnp.sqrt(a * a + b * b)
        cosine, sine = a * inv_radius, b * inv_radius
        cosines.append(cosine)
        sines.append(sine)
        column[j] = cosine * a + sine * b
        upper.append(column[: j + 1])
        target.append(-sine * target[j])
        target[j] = cosine * target[j]
    weights = [None] * KRYLOV
    for j in reversed(range(KRYLOV)):
        known = target[j]
        for k in range(j + 1, KRYLOV):
            known = known - upper[k][j] * weights[k]
        weights[j] = known / upper[j][j]
    out = []
    for k in range(KRYLOV):
        total = None
        for j in range(k, KRYLOV):
            term = weights[j] * basis[j][k]
            total = term if total is None else total + term
        out.append(total)
    return out


def kernel(
    ice_ref, owner_ref, slot_ref, vel_ref, wind_ref, strength_ref, mass_ref,
    out_ref, held_ref,
    st_vel, st_wind, st_strength, st_mass,
    fields, local, coef, stress, krylov,
    pack_e, pack_w, got_l, got_r, sums,
    buf_a, buf_b, send_blocks, recv_blocks, sum_blocks,
    in_sem, halo_send, halo_recv, ar_send, ar_recv, held_send, held_recv,
):
    lat, lon = lax.axis_index("lat"), lax.axis_index("lon")
    north, south = lax.rem(lat + LAT - 1, LAT), lax.rem(lat + 1, LAT)
    east, west = lax.rem(lon + 1, LON), lax.rem(lon + LON - 1, LON)
    core = lax.rem(lon, 2)
    chip = lon // 2
    rank_b = lat * 16 + chip
    y, z = chip // 4, lax.rem(chip, 4)

    partner = (lat, chip * 2 + (1 - core))
    peers_b = []
    shifts = [(i, j, k) for i in range(4) for j in range(4) for k in range(4) if i or j or k]
    for i, j, k in sorted(shifts, key=lambda d: -sum(min(n, 4 - n) + (n > 0) for n in d)):
        other = lax.rem(y + j, 4) * 4 + lax.rem(z + k, 4)
        peers_b.append((lax.rem(lat + i, 4), other * 2 + core))
    halo_peers = [(lat, east), (lat, west), (north, east), (north, west), (south, east), (south, west)]

    loads = []
    for t in range(2):
        cols = pl.ds(128 * t, 128)
        loads.append(pltpu.make_async_copy(vel_ref.at[:, :, cols], st_vel.at[:, t], in_sem.at[t]))
        loads.append(pltpu.make_async_copy(wind_ref.at[:, :, cols], st_wind.at[:, t], in_sem.at[2 + t]))
        loads.append(pltpu.make_async_copy(strength_ref.at[:, cols], st_strength.at[t], in_sem.at[4 + t]))
        loads.append(pltpu.make_async_copy(mass_ref.at[:, cols], st_mass.at[t], in_sem.at[6 + t]))
    for copy in loads:
        copy.start()

    barrier = pltpu.get_barrier_semaphore()
    greeted = peers_b + halo_peers
    for peer in greeted:
        pl.semaphore_signal(barrier, inc=1, device_id=peer, device_id_type=MESH)

    for copy in loads:
        copy.wait()

    ice = [[ice_ref[i, j].astype(F32) for j in range(2)] for i in range(2)]
    for half in range(2):

        def prepare(s, carry, half=half):
            src = pl.ds(pl.multiple_of(32 * s, 32), 32)
            dst = pl.ds(pl.multiple_of(TOP + 32 * s, 32), 32)
            lane = lanes((32, 128))
            for t in range(2):
                w = ice[half][t]
                mass = st_mass[t, src, :] * w
                v_e = st_vel[0, t, src, :]
                v_n = st_vel[1, t, src, :]
                values = (
                    v_e * w,
                    v_n * w,
                    st_strength[t, src, :] * w,
                    mass,
                    mass * v_e + w * st_wind[0, t, src, :],
                    mass * v_n + w * st_wind[1, t, src, :],
                )
                for f in range(6):
                    fields[f, t, dst, :] = values[f]
                local[0, t, dst, :] = mass + 0.5 * w
                local[1, t, dst, :] = 0.3 * mass
                local[2, t, dst, :] = jnp.zeros((32, 128), F32) + 0.5 * w
                packed = None
                for f in range(6):
                    turn = (OFFSETS[f] if t == 0 else OFFSETS[f] + WIDTHS[f]) % 128
                    rolled = values[f] if turn == 0 else pltpu.roll(values[f], turn, 1)
                    packed = rolled if f == 0 else jnp.where(lane >= OFFSETS[f], rolled, packed)
                (pack_w if t == 0 else pack_e)[src, :] = packed
            return carry

        lax.fori_loop(4 * half, 4 * half + 4, prepare, 0)

    first, second, both = pl.ds(0, 3), pl.ds(3, 3), pl.ds(0, 2)
    def reduce_a_start(inst, row):
        buf_a[inst, core] = row
        pltpu.make_async_remote_copy(
            src_ref=buf_a.at[inst, core], dst_ref=buf_a.at[inst, core],
            send_sem=ar_send.at[inst, 0], recv_sem=ar_recv.at[inst, 0],
            device_id=partner, device_id_type=MESH,
        ).start()

    def reduce_b_start(inst):
        waited = buf_a.at[inst, 0]
        pltpu.make_async_copy(waited, waited, ar_recv.at[inst, 0]).wait()
        buf_b[inst, rank_b] = buf_a[inst, 0] + buf_a[inst, 1]
        for peer in peers_b:
            pltpu.make_async_remote_copy(
                src_ref=buf_b.at[inst, rank_b], dst_ref=buf_b.at[inst, rank_b],
                send_sem=ar_send.at[inst, 1], recv_sem=ar_recv.at[inst, 1],
                device_id=peer, device_id_type=MESH,
            ).start()

    def reduce_end(inst):
        waited = buf_b.at[inst, pl.ds(0, 63)]
        pltpu.make_async_copy(waited, waited, ar_recv.at[inst, 1]).wait()
        parts = [buf_b[inst, pl.ds(8 * i, 8)] for i in range(8)]
        while len(parts) > 1:
            parts = [x + y for x, y in zip(parts[::2], parts[1::2])]
        return jnp.sum(parts[0], axis=0)

    def put_sum(index, acc):
        sums[index : index + 1, :] = jnp.sum(acc, axis=0, keepdims=True)

    def packed_sums(count):
        m = sums[0:count, :]
        total = jnp.sum(m, axis=1, keepdims=True)
        sub = lax.broadcasted_iota(jnp.int32, (count, 128), 0)
        spread = jnp.where(lanes((count, 128)) == sub, total, 0.0)
        return jnp.sum(spread, axis=0, keepdims=True)

    def estimate_pass(alpha, count):
        def at(c, r):
            flow = fields[c, both, rows8(r), :]
            return flow if alpha is None else flow + alpha * krylov[0, c, both, rows8(r), :]

        def one(r, carry):
            diag_acc, spread_acc, ice_acc = carry
            x_e, x_n = diff_x_rough(at(0, r)), diff_x_rough(at(1, r))
            y_e, y_n = at(0, r + 1) - at(0, r - 1), at(1, r + 1) - at(1, r - 1)
            m2, _, gs, gf, ge = coefficients(x_e + y_n, x_e - y_n, y_e + x_n, fields[2, both, rows8(r), :])
            diag, spread = spectrum_sums(
                m2, gs, gf, ge, local[0, both, rows8(r), :], local[1, both, rows8(r), :]
            )
            weight = local[2, both, rows8(r), :]
            return (
                diag_acc + (diag[0] + diag[1]),
                spread_acc + (spread[0] + spread[1]),
                ice_acc + 2.0 * (weight[0] + weight[1]),
            )

        def body(i, carry):
            for j in range(5):
                carry = one(pl.multiple_of(TOP + 8 + 48 * j + 16 * i, 8), carry)
            return carry

        zero = jnp.zeros((8, 128), F32)
        return lax.fori_loop(0, count, body, (zero, zero, zero))

    def basis_of(row, at):
        diag, spread, count = splat(row, at), splat(row, at + 1), splat(row, at + 2)
        inv = 1.0 / jnp.maximum(count, 1.0)
        mid = diag * inv
        return mid, jnp.maximum(spread * inv - mid * mid, 0.01)

    for i, acc in enumerate(estimate_pass(None, 3)):
        put_sum(i, acc)
    first_sums = packed_sums(8)

    pl.semaphore_wait(barrier, len(greeted))

    own_top, own_bot = pl.ds(TOP, HALO), pl.ds(BOT - HALO, HALO)
    halo_top, halo_bot = pl.ds(TOP - HALO, HALO), pl.ds(BOT, HALO)
    own_rows = pl.ds(TOP, 256)
    src_top, src_bot = pl.ds(0, HALO), pl.ds(256 - HALO, HALO)
    plan = [
        (fields.at[first, both, own_top, :], fields.at[first, both, halo_bot, :], (north, lon)),
        (fields.at[first, both, own_bot, :], fields.at[first, both, halo_top, :], (south, lon)),
        (pack_e.at[src_top, :], got_l.at[halo_bot, :], (north, east)),
        (pack_w.at[src_top, :], got_r.at[halo_bot, :], (north, west)),
        (pack_e, got_l.at[own_rows, :], (lat, east)),
        (pack_w, got_r.at[own_rows, :], (lat, west)),
        (pack_e.at[src_bot, :], got_l.at[halo_top, :], (south, east)),
        (pack_w.at[src_bot, :], got_r.at[halo_top, :], (south, west)),
        (fields.at[second, both, own_top, :], fields.at[second, both, halo_bot, :], (north, lon)),
        (fields.at[second, both, own_bot, :], fields.at[second, both, halo_top, :], (south, lon)),
    ]
    halo_copies = [None] * 10
    for i in (2, 3, 6, 7, 0, 1, 4, 5, 8, 9):
        src, dst, peer = plan[i]
        copy = pltpu.make_async_remote_copy(
            src_ref=src, dst_ref=dst, send_sem=halo_send.at[i], recv_sem=halo_recv.at[i],
            device_id=peer, device_id_type=MESH,
        )
        copy.start()
        halo_copies[i] = copy

    reduce_a_start(0, first_sums)

    keep_top = jnp.where(lat == 0, 0.0, 1.0).astype(F32)
    keep_bot = jnp.where(lat == LAT - 1, 0.0, 1.0).astype(F32)

    def put_local(t, here, mass):
        w = jnp.where(mass > 0.0, 1.0, 0.0)
        local[0, t, here, :] = mass + 0.5 * w
        local[1, t, here, :] = 0.3 * mass
        local[2, t, here, :] = 0.5 * w

    def unpack(keep):
        def body(r, n, carry):
            here = pl.ds(r, n)
            left, right = got_l[here, :], got_r[here, :]
            lane = lanes((n, 128))
            for f in range(6):
                turn_l = (128 - OFFSETS[f] - WIDTHS[f]) % 128
                turn_r = (128 - OFFSETS[f]) % 128
                from_l = left if turn_l == 0 else pltpu.roll(left, turn_l, 1)
                from_r = right if turn_r == 0 else pltpu.roll(right, turn_r, 1)
                merged = jnp.where(lane < 64, from_r, from_l)
                if keep is not None:
                    merged = merged * keep
                fields[f, 2, here, :] = merged
                if f == 3:
                    put_local(2, here, merged)
            return carry

        return body

    def clear_first(top, keep):
        fields[first, both, pl.ds(top, HALO), :] = fields[first, both, pl.ds(top, HALO), :] * keep

    def clear_second(top, keep):
        here = pl.ds(top, HALO)
        for t in range(2):
            for f in range(3, 6):
                kept = fields[f, t, here, :] * keep
                fields[f, t, here, :] = kept
                if f == 3:
                    put_local(t, here, kept)

    for copy in halo_copies[4:6]:
        copy.wait_recv()
    sweep(3, 35, unpack(None), 0, 4)
    for copy in halo_copies[:2]:
        copy.wait_recv()
    clear_first(TOP - HALO, keep_top)
    clear_first(BOT, keep_bot)

    def strips(halo):
        return 3 - halo, 35 + halo

    def viscous_pass(lo, hi):
        def body(r, n, carry):
            here, up, down = pl.ds(r, n), pl.ds(r + 1, n), pl.ds(r - 1, n)
            x_e, x_n = diff_x(fields[0, :, here, :]), diff_x(fields[1, :, here, :])
            y_e = fields[0, :, up, :] - fields[0, :, down, :]
            y_n = fields[1, :, up, :] - fields[1, :, down, :]
            pressure = fields[2, :, here, :]
            total, differ, shear = x_e + y_n, x_e - y_n, y_e + x_n
            values = coefficients(total, differ, shear, pressure)
            for i in range(5):
                coef[i, :, here, :] = values[i]
            p, n = values[0] * total - 0.5 * pressure, values[1] * differ
            stress[0, :, here, :] = p + n
            stress[1, :, here, :] = p - n
            stress[2, :, here, :] = values[1] * shear
            return carry

        sweep(lo, hi, body, 0, VISC)

    def tangent_pass(k, halo):
        def body(r, n, carry):
            here, up, down = pl.ds(r, n), pl.ds(r + 1, n), pl.ds(r - 1, n)
            x_e, x_n = diff_x(krylov[k, 0, :, here, :]), diff_x(krylov[k, 1, :, here, :])
            y_e = krylov[k, 0, :, up, :] - krylov[k, 0, :, down, :]
            y_n = krylov[k, 1, :, up, :] - krylov[k, 1, :, down, :]
            total, differ, shear = x_e + y_n, x_e - y_n, y_e + x_n
            gs, gf, ge = coef[2, :, here, :], coef[3, :, here, :], coef[4, :, here, :]
            q = gs * total + gf * differ + ge * shear
            m8 = coef[1, :, here, :]
            p = coef[0, :, here, :] * total - q * gs
            n = m8 * differ - q * gf
            stress[0, :, here, :] = p + n
            stress[1, :, here, :] = p - n
            stress[2, :, here, :] = m8 * shear - q * ge
            return carry

        lo, hi = strips(halo)
        sweep(lo, hi, body, 0, TAN)

    def stress_force(r, n):
        here, up, down = pl.ds(r, n), pl.ds(r + 1, n), pl.ds(r - 1, n)
        t11, t12 = stress[0, :, here, :], stress[2, :, here, :]
        y12 = stress[2, :, up, :] - stress[2, :, down, :]
        y22 = stress[1, :, up, :] - stress[1, :, down, :]
        half = local[2, :, here, :]
        return half * (diff_x(t11) + y12), half * (diff_x(t12) + y22)

    def residual_at(r, n):
        here = pl.ds(r, n)
        force_e, force_n = stress_force(r, n)
        mass, turn = local[0, :, here, :], local[1, :, here, :]
        a, b = fields[0, :, here, :], fields[1, :, here, :]
        r_e = fields[4, :, here, :] + force_e - (mass * a - turn * b)
        r_n = fields[5, :, here, :] + force_n - (mass * b + turn * a)
        return r_e, r_n

    def jacobian_at(k, r, n, mid, rho):
        here = pl.ds(r, n)
        force_e, force_n = stress_force(r, n)
        mass, turn = local[0, :, here, :] - mid, local[1, :, here, :]
        c, d = krylov[k, 0, :, here, :], krylov[k, 1, :, here, :]
        w_e = (mass * c - turn * d) - force_e
        w_n = (mass * d + turn * c) - force_n
        if k > 0:
            w_e = w_e - rho * krylov[k - 1, 0, :, here, :]
            w_n = w_n - rho * krylov[k - 1, 1, :, here, :]
        return w_e, w_n

    def vector_pass(make, k, halo):
        stored = k < KRYLOV

        def put(r, n):
            v_e, v_n = make(r, n)
            if stored:
                krylov[k, 0, :, pl.ds(r, n), :] = v_e
                krylov[k, 1, :, pl.ds(r, n), :] = v_n
            return v_e, v_n

        def outer(r, n, carry):
            put(r, n)
            return carry

        def inner(r, n, accs):
            v_e, v_n = put(r, n)
            v_e, v_n = v_e[:2], v_n[:2]
            out = []
            for i in range(k + 1):
                if i < k:
                    u_e = krylov[i, 0, pl.ds(0, 2), pl.ds(r, n), :]
                    u_n = krylov[i, 1, pl.ds(0, 2), pl.ds(r, n), :]
                else:
                    u_e, u_n = v_e, v_n
                out.append(accs[i] + fold(u_e * v_e + u_n * v_n))
            return tuple(out)

        lo, hi = strips(halo)
        if halo:
            sweep(lo, 3, outer, 0, halo)
        accs = sweep(3, 35, inner, tuple(jnp.zeros((8, 128), F32) for _ in range(k + 1)), VEC)
        if halo:
            sweep(35, hi, outer, 0, halo)
        return accs

    def dot_index(i, k):
        return k * (k + 1) // 2 + i

    mid = square = None
    for step in range(2):
        if step == 0:
            viscous_pass(4, 34)
            for copy in halo_copies[2:4] + halo_copies[6:8]:
                copy.wait_recv()
            sweep(0, 3, unpack(keep_top), 0, 3)
            sweep(35, 38, unpack(keep_bot), 0, 3)
            reduce_b_start(0)
            viscous_pass(0, 4)
            viscous_pass(34, 38)
        else:
            viscous_pass(*strips(2))
        if step == 0:
            for copy in halo_copies[8:]:
                copy.wait_recv()
            clear_second(TOP - HALO, keep_top)
            clear_second(BOT, keep_bot)
        accs = vector_pass(residual_at, 0, 3 - step)
        put_sum(0, accs[0])
        if step == 0:
            mid, square = basis_of(reduce_end(0), 0)
        rho = [None, 2.0 * square] + [square] * 3
        mid8, rho8 = mid, rho
        norm0 = accs[0]
        for k in range(KRYLOV):
            tangent_pass(k, ((3, 3, 2, 2, 1), (2, 1, 1, 1, 1))[step][k])
            accs = vector_pass(
                lambda r, n, k=k: jacobian_at(k, r, n, mid8, rho8[k]), k + 1, ((3, 2, 2, 2, 0), (1, 1, 1, 1, 0))[step][k]
            )
            for i, acc in enumerate(accs):
                put_sum(dot_index(i, k + 1), acc)
            if step == 0 and k == 0:
                def whole(acc):
                    return jnp.sum(jnp.sum(acc, axis=0, keepdims=True), axis=1, keepdims=True)

                g00, g01, g11 = whole(norm0), whole(accs[0]), whole(accs[1])
                m1 = mid[:, 0:1]
                alpha = (g01 + m1 * g00) / (g11 + 2.0 * m1 * g01 + m1 * m1 * g00 + 1e-12)
                alpha = jnp.broadcast_to(alpha, (8, 128))
                for i, acc in enumerate(estimate_pass(alpha, 1)):
                    put_sum(N_DOTS + i, acc)

        reduce_a_start(1 + step, packed_sums(N_SUMS))
        reduce_b_start(1 + step)
        row = reduce_end(1 + step)
        gram = [[None] * 6 for _ in range(6)]
        for j in range(6):
            for i in range(j + 1):
                gram[i][j] = gram[j][i] = splat(row, dot_index(i, j))
        weights = small_solve(gram, mid, rho)

        def update(r, n, carry, step=step, weights=weights):
            tiles = pl.ds(0, 3 if step == 0 else 2)
            for c in range(2):
                total = fields[c, tiles, pl.ds(r, n), :]
                for k in range(KRYLOV):
                    total = total + weights[k] * krylov[k, c, tiles, pl.ds(r, n), :]
                if step == 0:
                    fields[c, tiles, pl.ds(r, n), :] = total
                else:
                    for t in range(2):
                        out_ref[c, pl.ds(r - TOP, n), pl.ds(128 * t, 128)] = total[t]
            return carry

        if step == 0:
            for copy in halo_copies:
                copy.wait_send()
        lo, hi = strips(2 if step == 0 else 0)
        sweep(lo, hi, update, 0, UPD)
        if step == 0:
            mid, square = basis_of(row, N_DOTS)

    picks = []
    for s in range(8):
        picks.append([])
        for i in range(2):
            for j in range(2):
                hit = (ice_ref[i, j] > 0) & (owner_ref[i, j] * 2 + slot_ref[i, j] == s)
                picks[-1].append(jnp.where(hit, 1.0, 0.0).astype(F32))

    def choose(s, carry):
        src = pl.ds(pl.multiple_of(16 * s, 16), 16)
        for c in range(2):
            blocks = []
            for i in range(2):
                for j in range(2):
                    blocks.append(out_ref[c, pl.ds(pl.multiple_of(128 * i + 16 * s, 16), 16), pl.ds(128 * j, 128)])
            for slot in range(8):
                total = blocks[0] * picks[slot][0]
                for b in range(1, 4):
                    total = total + blocks[b] * picks[slot][b]
                send_blocks[slot // 2, slot % 2, c, src, :] = total
        return carry

    lax.fori_loop(0, 8, choose, 0)

    opposite = lax.rem(lat + 2, LAT)

    def held_copy(i, src, peer):
        copy = pltpu.make_async_remote_copy(
            src_ref=src, dst_ref=recv_blocks.at[i], send_sem=held_send.at[i], recv_sem=held_recv.at[i],
            device_id=(peer, lon), device_id_type=MESH,
        )
        copy.start()
        return copy

    held_copies = [
        held_copy(0, send_blocks.at[opposite, 0], south),
        held_copy(1, send_blocks.at[opposite, 1], north),
        held_copy(2, send_blocks.at[south, 1], south),
        held_copy(3, send_blocks.at[north, 0], north),
    ]

    def merge(i, owner, slot):
        def body(s, carry):
            r = pl.ds(pl.multiple_of(32 * s, 32), 32)
            for c in range(2):
                sum_blocks[i, c, r, :] = recv_blocks[i, c, r, :] + send_blocks[owner, slot, c, r, :]
            return carry

        lax.fori_loop(0, 4, body, 0)

    held_copies[0].wait_recv()
    merge(0, south, 0)
    held_copies.append(held_copy(4, sum_blocks.at[0], south))
    held_copies[1].wait_recv()
    merge(1, north, 1)
    held_copies.append(held_copy(5, sum_blocks.at[1], north))
    for copy in held_copies[2:]:
        copy.wait_recv()

    def collect(s, carry):
        r = pl.ds(pl.multiple_of(32 * s, 32), 32)
        for c in range(2):
            held_ref[0, 0, c, r, :] = send_blocks[lat, 0, c, r, :] + (recv_blocks[3, c, r, :] + recv_blocks[4, c, r, :])
            held_ref[1, 0, c, r, :] = send_blocks[lat, 1, c, r, :] + (recv_blocks[2, c, r, :] + recv_blocks[5, c, r, :])
        return carry

    lax.fori_loop(0, 4, collect, 0)

    for copy in held_copies:
        copy.wait_send()
    for inst in range(3):
        sent = buf_a.at[inst, 0]
        pltpu.make_async_copy(sent, sent, ar_send.at[inst, 0]).wait()
        sent = buf_b.at[inst, pl.ds(0, 63)]
        pltpu.make_async_copy(sent, sent, ar_send.at[inst, 1]).wait()


def on_device(velocity_old, wind_stress, strength, ice_mass, ice_mask, block_owner, block_slot):
    smem = pl.BlockSpec(memory_space=pltpu.SMEM)
    hbm = pl.BlockSpec(memory_space=pl.ANY)
    vm = pl.BlockSpec(memory_space=pltpu.VMEM)
    field = (3, ROWS, 128)
    velocity, held = pl.pallas_call(
        kernel,
        out_shape=(pltpu.VMEM((2, 256, 256), F32), pltpu.VMEM((2, 1, 2, 128, 128), F32)),
        in_specs=[smem] * 3 + [pl.BlockSpec(memory_space=pltpu.HBM)] * 4,
        out_specs=(vm, vm),
        scratch_shapes=[
            pltpu.VMEM((2, 2, 256, 128), F32),
            pltpu.VMEM((2, 2, 256, 128), F32),
            pltpu.VMEM((2, 256, 128), F32),
            pltpu.VMEM((2, 256, 128), F32),
            pltpu.VMEM((6,) + field, F32),
            pltpu.VMEM((3,) + field, F32),
            pltpu.VMEM((5,) + field, F32),
            pltpu.VMEM((3,) + field, F32),
            pltpu.VMEM((KRYLOV, 2) + field, F32),
            pltpu.VMEM((256, 128), F32),
            pltpu.VMEM((256, 128), F32),
            pltpu.VMEM((ROWS, 128), F32),
            pltpu.VMEM((ROWS, 128), F32),
            pltpu.VMEM((N_SUMS, 128), F32),
            pltpu.VMEM((3, 2, 1, 128), F32),
            pltpu.VMEM((3, 64, 1, 128), F32),
            pltpu.VMEM((4, 2, 2, 128, 128), F32),
            pltpu.VMEM((6, 2, 128, 128), F32),
            pltpu.VMEM((2, 2, 128, 128), F32),
            pltpu.SemaphoreType.DMA((8,)),
            pltpu.SemaphoreType.DMA((10,)),
            pltpu.SemaphoreType.DMA((10,)),
            pltpu.SemaphoreType.DMA((3, 2)),
            pltpu.SemaphoreType.DMA((3, 2)),
            pltpu.SemaphoreType.DMA((6,)),
            pltpu.SemaphoreType.DMA((6,)),
        ],
        compiler_params=pltpu.CompilerParams(
            collective_id=0, has_side_effects=True, vmem_limit_bytes=56 * 1024 * 1024
        ),
    )(ice_mask, block_owner, block_slot, velocity_old, wind_stress, strength, ice_mass)

    def pass_on(velocity_ref, held_ref, velocity_out, held_out, sem):
        copies = [
            pltpu.make_async_copy(velocity_ref, velocity_out, sem.at[0]),
            pltpu.make_async_copy(held_ref, held_out, sem.at[1]),
        ]
        for copy in copies:
            copy.start()
        for copy in copies:
            copy.wait()

    return pl.pallas_call(
        pass_on,
        out_shape=(
            jax.ShapeDtypeStruct((2, 256, 256), F32),
            jax.ShapeDtypeStruct((2, 1, 2, 128, 128), F32),
        ),
        in_specs=[hbm] * 2,
        out_specs=(hbm, hbm),
        scratch_shapes=[pltpu.SemaphoreType.DMA((2,))],
        compiler_params=pltpu.CompilerParams(vmem_limit_bytes=4 * 1024 * 1024),
    )(velocity, held)


def solution(mesh):
    return jax.shard_map(
        on_device,
        mesh=mesh,
        in_specs=(
            P(None, "lat", "lon"),
            P(None, "lat", "lon"),
            P("lat", "lon"),
            P("lat", "lon"),
            P("lat", "lon"),
            P("lat", "lon"),
            P("lat", "lon"),
        ),
        out_specs=(P(None, "lat", "lon"), P("lat", "lon", None, None, None)),
        check_vma=False,
    )
```

```python
import functools

import jax
import jax.numpy as jnp
from jax import lax
from jax.experimental import pallas as pl
from jax.experimental.pallas import tpu as pltpu
from jax.sharding import PartitionSpec as P

MESH = pl.DeviceIdType.MESH
F32 = jnp.float32

KRYLOV = 5
TINY_SQ = 1e-6
LAT = 4
LON = 32

ROWS = 320
TOP = 32
BOT = 288
HALO = 24
OWN_STRIPS = 32

WIDTHS = (22, 22, 22, 20, 20, 20)
OFFSETS = (0, 22, 44, 66, 86, 106)

VISC = 15
TAN = 19
VEC = 32
UPD = 4
SUB = 2

N_DOTS = 21
N_SUMS = 24


def lanes(shape):
    return lax.broadcasted_iota(jnp.int32, shape, len(shape) - 1)


def sweep(lo, hi, body, carry, strips):
    count, rest = divmod(hi - lo, strips)

    def step(i, carry):
        first = pl.multiple_of(8 + 8 * lo + 8 * strips * i, 8)
        for j in range(0, strips, SUB):
            carry = body(first + 8 * j, 8 * min(SUB, strips - j), carry)
        return carry

    if count:
        carry = lax.fori_loop(0, count, step, carry)
    if rest:
        carry = body(8 + 8 * (hi - rest), 8 * rest, carry)
    return carry


def fold(x):
    x = x.reshape(-1, 8, 128)
    total = x[0]
    for i in range(1, x.shape[0]):
        total = total + x[i]
    return total


def rows8(start):
    return pl.ds(start, 8)


def diff_x(f):
    lane = lanes((1,) + f.shape[1:])
    right = pltpu.roll(f, 127, 2)
    left = pltpu.roll(f, 1, 2)
    right_next = jnp.concatenate([right[1:], right[:1]], axis=0)
    left_next = jnp.concatenate([left[2:], left[:2]], axis=0)
    return jnp.where(lane == 127, right_next, right) - jnp.where(lane == 0, left_next, left)


def diff_x_rough(f):
    return pltpu.roll(f, 127, 2) - pltpu.roll(f, 1, 2)


def coefficients(sum_rate, differ, shear, pressure):
    q = 0.25 * (sum_rate * sum_rate) + 0.0625 * (differ * differ + shear * shear)
    inv = lax.rsqrt(q + 0.04)
    bulk = 0.5 * pressure * inv
    weight = inv * jnp.sqrt(0.5 * bulk)
    eighth = 0.125 * weight
    return 0.5 * bulk, 0.125 * bulk, (0.5 * weight) * sum_rate, eighth * differ, eighth * shear


def spectrum_sums(m2, gs, gf, ge, mass, turn):
    diag = mass + 1.5 * m2 - (gs * gs + gf * gf + ge * ge)
    c11 = 2.5 * m2 - 2.0 * (gs + gf) * (gs + gf)
    c22 = 2.5 * m2 - 2.0 * (gs - gf) * (gs - gf)
    c33 = 2.0 * m2 - 8.0 * ge * ge
    spread = diag * diag + turn * turn + 0.0625 * (c11 * c11 + c22 * c22) + 0.03125 * (c33 * c33)
    return diag, spread


def splat(row, index):
    return jnp.broadcast_to(row[:, index : index + 1], (1, 128))


def wide(row):
    return jnp.broadcast_to(row, (8, 128))


def small_solve(gram, mid, rho):
    def dot(u, gv):
        total = None
        for x, y in zip(u, gv):
            if x is not None:
                total = x * y if total is None else total + x * y
        return total

    def times_gram(u, count):
        return [dot(u, [gram[i][j] for j in range(6)]) for i in range(count)]

    def apply(c):
        out = [None] * 6
        for k, x in enumerate(c):
            if x is None:
                continue
            if k < 5:
                terms = [(k + 1, x), (k, mid * x)]
                if k > 0:
                    terms.append((k - 1, rho[k] * x))
                for at, term in terms:
                    out[at] = term if out[at] is None else out[at] + term
        return out

    beta = jnp.sqrt(gram[0][0] + TINY_SQ)
    basis = [[1.0 / beta] + [None] * 5]
    upper = []
    cosines, sines = [], []
    target = [beta]
    for j in range(KRYLOV):
        u = apply(basis[j])
        gu = times_gram(u, j + 2)
        coeffs = [dot(basis[i][: j + 2], gu) for i in range(j + 1)]
        for i in range(j + 1):
            u = [
                x if y is None else x - coeffs[i] * y
                for x, y in zip(u, basis[i])
            ]
        gu = times_gram(u, j + 2)
        square = jnp.maximum(dot(u[: j + 2], gu), 0.0)
        length = jnp.sqrt(square + TINY_SQ)
        inv_length = 1.0 / length
        basis.append([None if x is None else x * inv_length for x in u])
        column = coeffs + [length]
        for i in range(j):
            a, b = column[i], column[i + 1]
            column[i] = cosines[i] * a + sines[i] * b
            column[i + 1] = cosines[i] * b - sines[i] * a
        a, b = column[j], column[j + 1]
        inv_radius = 1.0 / jnp.sqrt(a * a + b * b)
        cosine, sine = a * inv_radius, b * inv_radius
        cosines.append(cosine)
        sines.append(sine)
        column[j] = cosine * a + sine * b
        upper.append(column[: j + 1])
        target.append(-sine * target[j])
        target[j] = cosine * target[j]
    weights = [None] * KRYLOV
    for j in reversed(range(KRYLOV)):
        known = target[j]
        for k in range(j + 1, KRYLOV):
            known = known - upper[k][j] * weights[k]
        weights[j] = known / upper[j][j]
    out = []
    for k in range(KRYLOV):
        total = None
        for j in range(k, KRYLOV):
            term = weights[j] * basis[j][k]
            total = term if total is None else total + term
        out.append(total)
    return out


def kernel(
    ice_ref, owner_ref, slot_ref, vel_ref, wind_ref, strength_ref, mass_ref,
    out_ref, held_ref,
    st_vel, st_wind, st_strength, st_mass,
    fields, local, coef, stress, krylov,
    pack_e, pack_w, got_l, got_r, sums,
    buf_a, buf_b, send_blocks, recv_blocks, sum_blocks,
    in_sem, halo_send, halo_recv, ar_send, ar_recv, held_send, held_recv,
):
    lat, lon = lax.axis_index("lat"), lax.axis_index("lon")
    north, south = lax.rem(lat + LAT - 1, LAT), lax.rem(lat + 1, LAT)
    east, west = lax.rem(lon + 1, LON), lax.rem(lon + LON - 1, LON)
    core = lax.rem(lon, 2)
    chip = lon // 2
    rank_b = lat * 16 + chip
    y, z = chip // 4, lax.rem(chip, 4)

    partner = (lat, chip * 2 + (1 - core))
    peers_b = []
    shifts = [(i, j, k) for i in range(4) for j in range(4) for k in range(4) if i or j or k]
    for i, j, k in sorted(shifts, key=lambda d: -sum(min(n, 4 - n) + (n > 0) for n in d)):
        other = lax.rem(y + j, 4) * 4 + lax.rem(z + k, 4)
        peers_b.append((lax.rem(lat + i, 4), other * 2 + core))
    halo_peers = [(lat, east), (lat, west), (north, east), (north, west), (south, east), (south, west)]

    loads = []
    for t in range(2):
        cols = pl.ds(128 * t, 128)
        loads.append(pltpu.make_async_copy(vel_ref.at[:, :, cols], st_vel.at[:, t], in_sem.at[t]))
        loads.append(pltpu.make_async_copy(wind_ref.at[:, :, cols], st_wind.at[:, t], in_sem.at[2 + t]))
        loads.append(pltpu.make_async_copy(strength_ref.at[:, cols], st_strength.at[t], in_sem.at[4 + t]))
        loads.append(pltpu.make_async_copy(mass_ref.at[:, cols], st_mass.at[t], in_sem.at[6 + t]))
    for copy in loads:
        copy.start()

    barrier = pltpu.get_barrier_semaphore()
    greeted = peers_b + halo_peers
    for peer in greeted:
        pl.semaphore_signal(barrier, inc=1, device_id=peer, device_id_type=MESH)

    for copy in loads:
        copy.wait()

    ice = [[ice_ref[i, j].astype(F32) for j in range(2)] for i in range(2)]
    for half in range(2):

        def prepare(s, carry, half=half):
            src = pl.ds(pl.multiple_of(32 * s, 32), 32)
            dst = pl.ds(pl.multiple_of(TOP + 32 * s, 32), 32)
            lane = lanes((32, 128))
            for t in range(2):
                w = ice[half][t]
                mass = st_mass[t, src, :] * w
                v_e = st_vel[0, t, src, :]
                v_n = st_vel[1, t, src, :]
                values = (
                    v_e * w,
                    v_n * w,
                    st_strength[t, src, :] * w,
                    mass,
                    mass * v_e + w * st_wind[0, t, src, :],
                    mass * v_n + w * st_wind[1, t, src, :],
                )
                for f in range(6):
                    fields[f, t, dst, :] = values[f]
                local[0, t, dst, :] = mass + 0.5 * w
                local[1, t, dst, :] = 0.3 * mass
                local[2, t, dst, :] = jnp.zeros((32, 128), F32) + 0.5 * w
                packed = None
                for f in range(6):
                    turn = (OFFSETS[f] if t == 0 else OFFSETS[f] + WIDTHS[f]) % 128
                    rolled = values[f] if turn == 0 else pltpu.roll(values[f], turn, 1)
                    packed = rolled if f == 0 else jnp.where(lane >= OFFSETS[f], rolled, packed)
                (pack_w if t == 0 else pack_e)[src, :] = packed
            return carry

        lax.fori_loop(4 * half, 4 * half + 4, prepare, 0)

    first, second, both = pl.ds(0, 3), pl.ds(3, 3), pl.ds(0, 2)
    def reduce_a_start(inst, row):
        buf_a[inst, core] = row
        pltpu.make_async_remote_copy(
            src_ref=buf_a.at[inst, core], dst_ref=buf_a.at[inst, core],
            send_sem=ar_send.at[inst, 0], recv_sem=ar_recv.at[inst, 0],
            device_id=partner, device_id_type=MESH,
        ).start()

    def reduce_b_start(inst):
        waited = buf_a.at[inst, 0]
        pltpu.make_async_copy(waited, waited, ar_recv.at[inst, 0]).wait()
        buf_b[inst, rank_b] = buf_a[inst, 0] + buf_a[inst, 1]
        for peer in peers_b:
            pltpu.make_async_remote_copy(
                src_ref=buf_b.at[inst, rank_b], dst_ref=buf_b.at[inst, rank_b],
                send_sem=ar_send.at[inst, 1], recv_sem=ar_recv.at[inst, 1],
                device_id=peer, device_id_type=MESH,
            ).start()

    def reduce_end(inst):
        waited = buf_b.at[inst, pl.ds(0, 63)]
        pltpu.make_async_copy(waited, waited, ar_recv.at[inst, 1]).wait()
        parts = [buf_b[inst, pl.ds(8 * i, 8)] for i in range(8)]
        while len(parts) > 1:
            parts = [x + y for x, y in zip(parts[::2], parts[1::2])]
        return jnp.sum(parts[0], axis=0)

    def put_sum(index, acc):
        sums[index : index + 1, :] = jnp.sum(acc, axis=0, keepdims=True)

    def packed_sums(count):
        m = sums[0:count, :]
        total = jnp.sum(m, axis=1, keepdims=True)
        sub = lax.broadcasted_iota(jnp.int32, (count, 128), 0)
        spread = jnp.where(lanes((count, 128)) == sub, total, 0.0)
        return jnp.sum(spread, axis=0, keepdims=True)

    def estimate_pass(alpha, count):
        def at(c, r):
            flow = fields[c, both, rows8(r), :]
            return flow if alpha is None else flow + alpha * krylov[0, c, both, rows8(r), :]

        def one(r, carry):
            diag_acc, spread_acc, ice_acc = carry
            x_e, x_n = diff_x_rough(at(0, r)), diff_x_rough(at(1, r))
            y_e, y_n = at(0, r + 1) - at(0, r - 1), at(1, r + 1) - at(1, r - 1)
            m2, _, gs, gf, ge = coefficients(x_e + y_n, x_e - y_n, y_e + x_n, fields[2, both, rows8(r), :])
            diag, spread = spectrum_sums(
                m2, gs, gf, ge, local[0, both, rows8(r), :], local[1, both, rows8(r), :]
            )
            weight = local[2, both, rows8(r), :]
            return (
                diag_acc + (diag[0] + diag[1]),
                spread_acc + (spread[0] + spread[1]),
                ice_acc + 2.0 * (weight[0] + weight[1]),
            )

        def body(i, carry):
            for j in range(5):
                carry = one(pl.multiple_of(TOP + 8 + 48 * j + 16 * i, 8), carry)
            return carry

        zero = jnp.zeros((8, 128), F32)
        return lax.fori_loop(0, count, body, (zero, zero, zero))

    def basis_of(row, at):
        diag, spread, count = splat(row, at), splat(row, at + 1), splat(row, at + 2)
        inv = 1.0 / jnp.maximum(count, 1.0)
        mid = diag * inv
        return mid, jnp.maximum(spread * inv - mid * mid, 0.01)

    for i, acc in enumerate(estimate_pass(None, 3)):
        put_sum(i, acc)
    first_sums = packed_sums(8)

    pl.semaphore_wait(barrier, len(greeted))

    own_top, own_bot = pl.ds(TOP, HALO), pl.ds(BOT - HALO, HALO)
    halo_top, halo_bot = pl.ds(TOP - HALO, HALO), pl.ds(BOT, HALO)
    own_rows = pl.ds(TOP, 256)
    src_top, src_bot = pl.ds(0, HALO), pl.ds(256 - HALO, HALO)
    plan = [
        (fields.at[first, both, own_top, :], fields.at[first, both, halo_bot, :], (north, lon)),
        (fields.at[first, both, own_bot, :], fields.at[first, both, halo_top, :], (south, lon)),
        (pack_e.at[src_top, :], got_l.at[halo_bot, :], (north, east)),
        (pack_w.at[src_top, :], got_r.at[halo_bot, :], (north, west)),
        (pack_e, got_l.at[own_rows, :], (lat, east)),
        (pack_w, got_r.at[own_rows, :], (lat, west)),
        (pack_e.at[src_bot, :], got_l.at[halo_top, :], (south, east)),
        (pack_w.at[src_bot, :], got_r.at[halo_top, :], (south, west)),
        (fields.at[second, both, own_top, :], fields.at[second, both, halo_bot, :], (north, lon)),
        (fields.at[second, both, own_bot, :], fields.at[second, both, halo_top, :], (south, lon)),
    ]
    halo_copies = [None] * 10
    for i in (2, 3, 6, 7, 0, 1, 4, 5, 8, 9):
        src, dst, peer = plan[i]
        copy = pltpu.make_async_remote_copy(
            src_ref=src, dst_ref=dst, send_sem=halo_send.at[i], recv_sem=halo_recv.at[i],
            device_id=peer, device_id_type=MESH,
        )
        copy.start()
        halo_copies[i] = copy

    reduce_a_start(0, first_sums)

    keep_top = jnp.where(lat == 0, 0.0, 1.0).astype(F32)
    keep_bot = jnp.where(lat == LAT - 1, 0.0, 1.0).astype(F32)

    def put_local(t, here, mass):
        w = jnp.where(mass > 0.0, 1.0, 0.0)
        local[0, t, here, :] = mass + 0.5 * w
        local[1, t, here, :] = 0.3 * mass
        local[2, t, here, :] = 0.5 * w

    def unpack(keep):
        def body(r, n, carry):
            here = pl.ds(r, n)
            left, right = got_l[here, :], got_r[here, :]
            lane = lanes((n, 128))
            for f in range(6):
                turn_l = (128 - OFFSETS[f] - WIDTHS[f]) % 128
                turn_r = (128 - OFFSETS[f]) % 128
                from_l = left if turn_l == 0 else pltpu.roll(left, turn_l, 1)
                from_r = right if turn_r == 0 else pltpu.roll(right, turn_r, 1)
                merged = jnp.where(lane < 64, from_r, from_l)
                if keep is not None:
                    merged = merged * keep
                fields[f, 2, here, :] = merged
                if f == 3:
                    put_local(2, here, merged)
            return carry

        return body

    def clear_first(top, keep):
        fields[first, both, pl.ds(top, HALO), :] = fields[first, both, pl.ds(top, HALO), :] * keep

    def clear_second(top, keep):
        here = pl.ds(top, HALO)
        for t in range(2):
            for f in range(3, 6):
                kept = fields[f, t, here, :] * keep
                fields[f, t, here, :] = kept
                if f == 3:
                    put_local(t, here, kept)

    for copy in halo_copies[4:6]:
        copy.wait_recv()
    sweep(3, 35, unpack(None), 0, 4)
    for copy in halo_copies[:2]:
        copy.wait_recv()
    clear_first(TOP - HALO, keep_top)
    clear_first(BOT, keep_bot)

    def strips(halo):
        return 3 - halo, 35 + halo

    def viscous_pass(lo, hi):
        def body(r, n, carry):
            here, up, down = pl.ds(r, n), pl.ds(r + 1, n), pl.ds(r - 1, n)
            x_e, x_n = diff_x(fields[0, :, here, :]), diff_x(fields[1, :, here, :])
            y_e = fields[0, :, up, :] - fields[0, :, down, :]
            y_n = fields[1, :, up, :] - fields[1, :, down, :]
            pressure = fields[2, :, here, :]
            total, differ, shear = x_e + y_n, x_e - y_n, y_e + x_n
            values = coefficients(total, differ, shear, pressure)
            for i in range(5):
                coef[i, :, here, :] = values[i]
            p, n = values[0] * total - 0.5 * pressure, values[1] * differ
            stress[0, :, here, :] = p + n
            stress[1, :, here, :] = p - n
            stress[2, :, here, :] = values[1] * shear
            return carry

        sweep(lo, hi, body, 0, VISC)

    def tangent_pass(k, halo):
        def body(r, n, carry):
            here, up, down = pl.ds(r, n), pl.ds(r + 1, n), pl.ds(r - 1, n)
            x_e, x_n = diff_x(krylov[k, 0, :, here, :]), diff_x(krylov[k, 1, :, here, :])
            y_e = krylov[k, 0, :, up, :] - krylov[k, 0, :, down, :]
            y_n = krylov[k, 1, :, up, :] - krylov[k, 1, :, down, :]
            total, differ, shear = x_e + y_n, x_e - y_n, y_e + x_n
            gs, gf, ge = coef[2, :, here, :], coef[3, :, here, :], coef[4, :, here, :]
            q = gs * total + gf * differ + ge * shear
            m8 = coef[1, :, here, :]
            p = coef[0, :, here, :] * total - q * gs
            n = m8 * differ - q * gf
            stress[0, :, here, :] = p + n
            stress[1, :, here, :] = p - n
            stress[2, :, here, :] = m8 * shear - q * ge
            return carry

        lo, hi = strips(halo)
        sweep(lo, hi, body, 0, TAN)

    def stress_force(r, n):
        here, up, down = pl.ds(r, n), pl.ds(r + 1, n), pl.ds(r - 1, n)
        t11, t12 = stress[0, :, here, :], stress[2, :, here, :]
        y12 = stress[2, :, up, :] - stress[2, :, down, :]
        y22 = stress[1, :, up, :] - stress[1, :, down, :]
        half = local[2, :, here, :]
        return half * (diff_x(t11) + y12), half * (diff_x(t12) + y22)

    def residual_at(r, n):
        here = pl.ds(r, n)
        force_e, force_n = stress_force(r, n)
        mass, turn = local[0, :, here, :], local[1, :, here, :]
        a, b = fields[0, :, here, :], fields[1, :, here, :]
        r_e = fields[4, :, here, :] + force_e - (mass * a - turn * b)
        r_n = fields[5, :, here, :] + force_n - (mass * b + turn * a)
        return r_e, r_n

    def jacobian_at(k, r, n, mid, rho):
        here = pl.ds(r, n)
        force_e, force_n = stress_force(r, n)
        mass, turn = local[0, :, here, :] - mid, local[1, :, here, :]
        c, d = krylov[k, 0, :, here, :], krylov[k, 1, :, here, :]
        w_e = (mass * c - turn * d) - force_e
        w_n = (mass * d + turn * c) - force_n
        if k > 0:
            w_e = w_e - rho * krylov[k - 1, 0, :, here, :]
            w_n = w_n - rho * krylov[k - 1, 1, :, here, :]
        return w_e, w_n

    def vector_pass(make, k, halo):
        stored = k < KRYLOV

        def put(r, n):
            v_e, v_n = make(r, n)
            if stored:
                krylov[k, 0, :, pl.ds(r, n), :] = v_e
                krylov[k, 1, :, pl.ds(r, n), :] = v_n
            return v_e, v_n

        def outer(r, n, carry):
            put(r, n)
            return carry

        def inner(r, n, accs):
            v_e, v_n = put(r, n)
            v_e, v_n = v_e[:2], v_n[:2]
            out = []
            for i in range(k + 1):
                if i < k:
                    u_e = krylov[i, 0, pl.ds(0, 2), pl.ds(r, n), :]
                    u_n = krylov[i, 1, pl.ds(0, 2), pl.ds(r, n), :]
                else:
                    u_e, u_n = v_e, v_n
                out.append(accs[i] + fold(u_e * v_e + u_n * v_n))
            return tuple(out)

        lo, hi = strips(halo)
        if halo:
            sweep(lo, 3, outer, 0, halo)
        accs = sweep(3, 35, inner, tuple(jnp.zeros((8, 128), F32) for _ in range(k + 1)), VEC)
        if halo:
            sweep(35, hi, outer, 0, halo)
        return accs

    def dot_index(i, k):
        return k * (k + 1) // 2 + i

    mid = square = None
    for step in range(2):
        if step == 0:
            viscous_pass(4, 34)
            for copy in halo_copies[2:4] + halo_copies[6:8]:
                copy.wait_recv()
            sweep(0, 3, unpack(keep_top), 0, 3)
            sweep(35, 38, unpack(keep_bot), 0, 3)
            reduce_b_start(0)
            viscous_pass(0, 4)
            viscous_pass(34, 38)
        else:
            viscous_pass(*strips(2))
        if step == 0:
            for copy in halo_copies[8:]:
                copy.wait_recv()
            clear_second(TOP - HALO, keep_top)
            clear_second(BOT, keep_bot)
        accs = vector_pass(residual_at, 0, 3 - step)
        put_sum(0, accs[0])
        if step == 0:
            mid, square = basis_of(reduce_end(0), 0)
        rho = [None, 2.0 * square] + [square] * 3
        mid8, rho8 = mid, rho
        norm0 = accs[0]
        for k in range(KRYLOV):
            tangent_pass(k, ((3, 3, 2, 2, 1), (2, 1, 1, 1, 1))[step][k])
            accs = vector_pass(
                lambda r, n, k=k: jacobian_at(k, r, n, mid8, rho8[k]), k + 1, ((3, 2, 2, 2, 0), (1, 1, 1, 1, 0))[step][k]
            )
            for i, acc in enumerate(accs):
                put_sum(dot_index(i, k + 1), acc)
            if step == 0 and k == 0:
                def whole(acc):
                    return jnp.sum(jnp.sum(acc, axis=0, keepdims=True), axis=1, keepdims=True)

                g00, g01, g11 = whole(norm0), whole(accs[0]), whole(accs[1])
                m1 = mid[:, 0:1]
                alpha = (g01 + m1 * g00) / (g11 + 2.0 * m1 * g01 + m1 * m1 * g00 + 1e-12)
                alpha = jnp.broadcast_to(alpha, (8, 128))
                for i, acc in enumerate(estimate_pass(alpha, 1)):
                    put_sum(N_DOTS + i, acc)

        reduce_a_start(1 + step, packed_sums(N_SUMS))
        reduce_b_start(1 + step)
        row = reduce_end(1 + step)
        gram = [[None] * 6 for _ in range(6)]
        for j in range(6):
            for i in range(j + 1):
                gram[i][j] = gram[j][i] = splat(row, dot_index(i, j))
        weights = small_solve(gram, mid, rho)

        def update(r, n, carry, step=step, weights=weights):
            tiles = pl.ds(0, 3 if step == 0 else 2)
            for c in range(2):
                total = fields[c, tiles, pl.ds(r, n), :]
                for k in range(KRYLOV):
                    total = total + weights[k] * krylov[k, c, tiles, pl.ds(r, n), :]
                if step == 0:
                    fields[c, tiles, pl.ds(r, n), :] = total
                else:
                    for t in range(2):
                        out_ref[c, pl.ds(r - TOP, n), pl.ds(128 * t, 128)] = total[t]
            return carry

        if step == 0:
            for copy in halo_copies:
                copy.wait_send()
        lo, hi = strips(2 if step == 0 else 0)
        sweep(lo, hi, update, 0, UPD)
        if step == 0:
            mid, square = basis_of(row, N_DOTS)

    picks = []
    for s in range(8):
        picks.append([])
        for i in range(2):
            for j in range(2):
                hit = (ice_ref[i, j] > 0) & (owner_ref[i, j] * 2 + slot_ref[i, j] == s)
                picks[-1].append(jnp.where(hit, 1.0, 0.0).astype(F32))

    def choose(s, carry):
        src = pl.ds(pl.multiple_of(16 * s, 16), 16)
        for c in range(2):
            blocks = []
            for i in range(2):
                for j in range(2):
                    blocks.append(out_ref[c, pl.ds(pl.multiple_of(128 * i + 16 * s, 16), 16), pl.ds(128 * j, 128)])
            for slot in range(8):
                total = blocks[0] * picks[slot][0]
                for b in range(1, 4):
                    total = total + blocks[b] * picks[slot][b]
                send_blocks[slot // 2, slot % 2, c, src, :] = total
        return carry

    lax.fori_loop(0, 8, choose, 0)

    opposite = lax.rem(lat + 2, LAT)

    def held_copy(i, src, peer):
        copy = pltpu.make_async_remote_copy(
            src_ref=src, dst_ref=recv_blocks.at[i], send_sem=held_send.at[i], recv_sem=held_recv.at[i],
            device_id=(peer, lon), device_id_type=MESH,
        )
        copy.start()
        return copy

    held_copies = [
        held_copy(0, send_blocks.at[opposite, 0], south),
        held_copy(1, send_blocks.at[opposite, 1], north),
        held_copy(2, send_blocks.at[south, 1], south),
        held_copy(3, send_blocks.at[north, 0], north),
    ]

    def merge(i, owner, slot):
        def body(s, carry):
            r = pl.ds(pl.multiple_of(32 * s, 32), 32)
            for c in range(2):
                sum_blocks[i, c, r, :] = recv_blocks[i, c, r, :] + send_blocks[owner, slot, c, r, :]
            return carry

        lax.fori_loop(0, 4, body, 0)

    held_copies[0].wait_recv()
    merge(0, south, 0)
    held_copies.append(held_copy(4, sum_blocks.at[0], south))
    held_copies[1].wait_recv()
    merge(1, north, 1)
    held_copies.append(held_copy(5, sum_blocks.at[1], north))
    for copy in held_copies[2:]:
        copy.wait_recv()

    def collect(s, carry):
        r = pl.ds(pl.multiple_of(32 * s, 32), 32)
        for c in range(2):
            held_ref[0, 0, c, r, :] = send_blocks[lat, 0, c, r, :] + (recv_blocks[3, c, r, :] + recv_blocks[4, c, r, :])
            held_ref[1, 0, c, r, :] = send_blocks[lat, 1, c, r, :] + (recv_blocks[2, c, r, :] + recv_blocks[5, c, r, :])
        return carry

    lax.fori_loop(0, 4, collect, 0)

    for copy in held_copies:
        copy.wait_send()
    for inst in range(3):
        sent = buf_a.at[inst, 0]
        pltpu.make_async_copy(sent, sent, ar_send.at[inst, 0]).wait()
        sent = buf_b.at[inst, pl.ds(0, 63)]
        pltpu.make_async_copy(sent, sent, ar_send.at[inst, 1]).wait()


def on_device(velocity_old, wind_stress, strength, ice_mass, ice_mask, block_owner, block_slot):
    smem = pl.BlockSpec(memory_space=pltpu.SMEM)
    hbm = pl.BlockSpec(memory_space=pl.ANY)
    vm = pl.BlockSpec(memory_space=pltpu.VMEM)
    field = (3, ROWS, 128)
    velocity, held = pl.pallas_call(
        kernel,
        out_shape=(pltpu.VMEM((2, 256, 256), F32), pltpu.VMEM((2, 1, 2, 128, 128), F32)),
        in_specs=[smem] * 3 + [pl.BlockSpec(memory_space=pltpu.HBM)] * 4,
        out_specs=(vm, vm),
        scratch_shapes=[
            pltpu.VMEM((2, 2, 256, 128), F32),
            pltpu.VMEM((2, 2, 256, 128), F32),
            pltpu.VMEM((2, 256, 128), F32),
            pltpu.VMEM((2, 256, 128), F32),
            pltpu.VMEM((6,) + field, F32),
            pltpu.VMEM((3,) + field, F32),
            pltpu.VMEM((5,) + field, F32),
            pltpu.VMEM((3,) + field, F32),
            pltpu.VMEM((KRYLOV, 2) + field, F32),
            pltpu.VMEM((256, 128), F32),
            pltpu.VMEM((256, 128), F32),
            pltpu.VMEM((ROWS, 128), F32),
            pltpu.VMEM((ROWS, 128), F32),
            pltpu.VMEM((N_SUMS, 128), F32),
            pltpu.VMEM((3, 2, 1, 128), F32),
            pltpu.VMEM((3, 64, 1, 128), F32),
            pltpu.VMEM((4, 2, 2, 128, 128), F32),
            pltpu.VMEM((6, 2, 128, 128), F32),
            pltpu.VMEM((2, 2, 128, 128), F32),
            pltpu.SemaphoreType.DMA((8,)),
            pltpu.SemaphoreType.DMA((10,)),
            pltpu.SemaphoreType.DMA((10,)),
            pltpu.SemaphoreType.DMA((3, 2)),
            pltpu.SemaphoreType.DMA((3, 2)),
            pltpu.SemaphoreType.DMA((6,)),
            pltpu.SemaphoreType.DMA((6,)),
        ],
        compiler_params=pltpu.CompilerParams(
            collective_id=0, has_side_effects=True, vmem_limit_bytes=56 * 1024 * 1024
        ),
    )(ice_mask, block_owner, block_slot, velocity_old, wind_stress, strength, ice_mass)

    def pass_on(velocity_ref, held_ref, velocity_out, held_out, sem):
        copies = [
            pltpu.make_async_copy(velocity_ref, velocity_out, sem.at[0]),
            pltpu.make_async_copy(held_ref, held_out, sem.at[1]),
        ]
        for copy in copies:
            copy.start()
        for copy in copies:
            copy.wait()

    return pl.pallas_call(
        pass_on,
        out_shape=(
            jax.ShapeDtypeStruct((2, 256, 256), F32),
            jax.ShapeDtypeStruct((2, 1, 2, 128, 128), F32),
        ),
        in_specs=[hbm] * 2,
        out_specs=(hbm, hbm),
        scratch_shapes=[pltpu.SemaphoreType.DMA((2,))],
        compiler_params=pltpu.CompilerParams(vmem_limit_bytes=4 * 1024 * 1024),
    )(velocity, held)


def solution(mesh):
    return jax.shard_map(
        on_device,
        mesh=mesh,
        in_specs=(
            P(None, "lat", "lon"),
            P(None, "lat", "lon"),
            P("lat", "lon"),
            P("lat", "lon"),
            P("lat", "lon"),
            P("lat", "lon"),
            P("lat", "lon"),
        ),
        out_specs=(P(None, "lat", "lon"), P("lat", "lon", None, None, None)),
        check_vma=False,
    )
```
